256 devices in a mesh: kv: 4 (over y), leaf: 64 (over x, z, core).
Axes of the slice: x: 4, y: 4, z: 8, core: 2. Of those that a mesh axis runs over, the one named last changes fastest.
Arguments:
- queries: bfloat16 [2, 256, 4, 2048], P(None, 'leaf', 'kv'), may hold values from -8 to 8
- query_gain: float32 [128], replicated, may hold values from 0.5 to 1.5
- new_keys: bfloat16 [2, 256, 4, 128], P(None, 'leaf', 'kv'), may hold values from -12 to 12
- new_values: bfloat16 [2, 256, 4, 128], P(None, 'leaf', 'kv'), may hold values from -6 to 6
- root_keys: bfloat16 [32768, 4, 128], P('leaf', 'kv'), may hold values from -40 to 40
- root_values: bfloat16 [32768, 4, 128], P('leaf', 'kv'), may hold values from -6 to 6
- branch_keys: bfloat16 [131072, 4, 128], P('leaf', 'kv'), may hold values from -9 to 9
- branch_values: bfloat16 [131072, 4, 128], P('leaf', 'kv'), may hold values from -6 to 6
- suffix_keys: bfloat16 [256, 512, 4, 128], P('leaf', None, 'kv'), may hold values from -9 to 9
- suffix_values: bfloat16 [256, 512, 4, 128], P('leaf', None, 'kv'), may hold values from -6 to 6
- out_weight: bfloat16 [8192, 4096], P('kv', 'leaf'), may hold values from -0.0625 to 0.0625
- request_branch: int32 [256], replicated, may hold values from 0 to 15
- branch_blocks: int32 [16], replicated, may hold values from 1 to 128, 512 in all
- suffix_length: int32 [256], P('leaf'), may hold values from 1 to 512, 65536 in all
- block_slot: int32 [512], replicated, may hold values from 0 to 511, each once
Outputs:
- attn_out: float32 [2, 256, 4, 2048], P(None, 'leaf', 'kv')
- log_total: float32 [2, 256, 4, 16], P(None, 'leaf', 'kv')
- layer_out: float32 [2, 256, 4096], P(None, 'kv', 'leaf')
The draws below stay inside these ranges and needn't reach their ends.
Inputs may be any that keep to these rules, and one draw needn't show every extreme that they name: `branch_blocks`: every branch has one block or more; they sum to 512; the largest is exactly 128. `suffix_length`: they sum to 65536; the largest is exactly 512. `block_slot`: a permutation of 0 .. 511.
All inputs are finite; a program needn't handle non-finite values. No bound on the sum of `suffix_length` on one device may be relied on, other than what follows from the above.
Results may differ from the reference program's by a relative error of at most 0.014.
Values may be sent and summed in bfloat16 or wider, within the bound.
No kernel may reach another device: no remote copies, remote signals or barrier semaphores. Data moves between devices by JAX's collectives and lax.ppermute only.
A program may use at most 64 MiB of HBM per device.

```python
import math
import jax
import jax.numpy as jnp
import numpy as np
from jax import lax

KVH = 4
GROUP = 16
HD = 128
D = 4096
BLK = 256
SUF = 512
STEPS = 2
BRANCHES = 16
REQUESTS = 256
ROOT = 32768
BLOCKS = 512


def draw_queries(key, part):
    key = jax.random.fold_in(key, 1)
    drawn_values = jnp.clip(jax.random.normal(key, (STEPS, REQUESTS, KVH, GROUP, HD), jnp.float32), -6.0, 6.0)
    return drawn_values.reshape(STEPS, REQUESTS, KVH, GROUP * HD).astype(jnp.bfloat16)


def draw_root_keys(key, part):
    key = jax.random.fold_in(key, 2)
    drawn_values = 1.5 * jnp.clip(jax.random.normal(key, (ROOT, KVH, HD), jnp.float32), -6.0, 6.0)
    return drawn_values.astype(jnp.bfloat16)


def touch_ends(result, rng, smallest, high):
    longest = result.shape.index(max(result.shape))
    spots = []
    for shift in (0, 1):
        where = [jax.random.randint(jax.random.fold_in(rng, axis), (), 0, length) for axis, length in enumerate(result.shape)]
        where[longest] = (where[longest] + shift) % result.shape[longest]
        spots.append(tuple(where))
    return result.at[spots[0]].set(smallest).at[spots[1]].set(high)


def level_of(own_key, extent, pieces, low, top_value):
    level = 1.0
    for dim, shards_of in pieces:
        steps = jax.random.uniform(jax.random.fold_in(jax.random.fold_in(own_key, 6), dim), (shards_of,), jnp.float32, low / len(pieces), top_value / len(pieces))
        level = level * jnp.repeat(jnp.exp(steps), extent[dim] // shards_of).reshape((-1,) + (1,) * (len(extent) - 1 - dim))
    return level


def rank_table(amount, slope):
    loads = [(1 << 20) // math.isqrt(rank ** slope) + 1 for rank in range(1, amount + 1)]
    width = 1 + sum(loads) // (1 << 30)
    return np.cumsum(np.array([max(1, weight // width) for weight in loads]))


def skewed_ids(own_key, dims, number_of, slope):
    listing = rank_table(number_of, slope)
    ticket = jax.random.randint(jax.random.fold_in(own_key, 1), dims, 0, int(listing[number_of - 1]))
    standing = jnp.searchsorted(jnp.asarray(listing, jnp.int32), ticket, side="right")
    return jax.random.permutation(jax.random.fold_in(own_key, 2), number_of)[standing].astype(jnp.int32)


def length_profile(amount, total, bound, skew):
    loads = [(1 << 20) // math.isqrt(rank ** skew) + 1 for rank in range(2, amount + 1)]
    rest, counts = total - bound - (amount - 1), [1] * (amount - 1)
    while rest > 0:
        movable = [i for i in range(amount - 1) if counts[i] < bound]
        pool, left = sum([loads[i] for i in movable]), rest
        for i in movable:
            addition = min(bound - counts[i], max(1, left * loads[i] // pool), rest)
            counts[i] = counts[i] + addition
            rest = rest - addition
    return np.array([bound] + counts)


def uneven_parts(stream_key, count, total, bound, lean):
    if count == 2:
        one = jax.random.randint(stream_key, (), max(1, total - bound), min(bound, total - 1) + 1)
        return jnp.stack([one, total - one])
    tallies = jnp.asarray(length_profile(count, total, bound, lean), jnp.int32)
    pairs = (count - 1) // 2
    source_of, taker = tallies[1:1 + 2 * pairs:2], tallies[2:2 + 2 * pairs:2]
    margin = jnp.minimum(source_of - 1, bound - taker)
    shifted = jax.random.randint(jax.random.fold_in(stream_key, 1), (pairs,), 0, 1 << 20) % (margin + 1)
    tallies = tallies.at[1:1 + 2 * pairs:2].set(source_of - shifted).at[2:2 + 2 * pairs:2].set(taker + shifted)
    return tallies[jax.random.permutation(jax.random.fold_in(stream_key, 2), count)]


def normal_values(rng, shape, deviation, bound, shards=(), held_as=jnp.bfloat16):
    values = deviation * jax.random.normal(rng, shape, jnp.float32)
    if shards:
        values = values * level_of(rng, shape, shards, -0.22, 0.18)
    return jnp.clip(values, -bound, bound).astype(held_as)


def setup_inputs(seed: int = 0) -> dict:
    splits = jax.random.split(jax.random.key(seed), 16)
    queries = draw_queries(jax.random.fold_in(splits[15], 71), 0)
    query_gain = jnp.clip(1.0 + 0.1 * jax.random.normal(splits[1], (HD,), jnp.float32), 0.5, 1.5)
    new_keys = normal_values(splits[2], (STEPS, REQUESTS, KVH, HD), 3.0, 12.0, ((1, 64), (2, 4)))
    new_values = normal_values(splits[3], (STEPS, REQUESTS, KVH, HD), 1.0, 6.0, ((1, 64), (2, 4)))
    root_keys = draw_root_keys(jax.random.fold_in(splits[15], 71), 0)
    root_values = normal_values(splits[5], (ROOT, KVH, HD), 1.0, 6.0, ((0, 64), (1, 4)))
    branch_keys = normal_values(splits[6], (BLOCKS * BLK, KVH, HD), 1.5, 9.0, ((0, 64), (1, 4)))
    branch_values = normal_values(splits[7], (BLOCKS * BLK, KVH, HD), 1.0, 6.0, ((0, 64), (1, 4)))
    suffix_keys = normal_values(splits[8], (REQUESTS, SUF, KVH, HD), 1.5, 9.0, ((0, 64), (2, 4)))
    suffix_values = normal_values(splits[9], (REQUESTS, SUF, KVH, HD), 1.0, 6.0, ((0, 64), (2, 4)))
    out_weight = normal_values(splits[10], (KVH * GROUP * HD, D), (KVH * GROUP * HD) ** -0.5, 0.0625, ((0, 4), (1, 64)))
    request_branch = touch_ends(skewed_ids(splits[11], (REQUESTS,), BRANCHES, 2), jax.random.fold_in(splits[11], 3), 0, BRANCHES - 1).astype(jnp.int32)
    branch_blocks = uneven_parts(splits[12], BRANCHES, BLOCKS, BLOCKS // 4, 2).astype(jnp.int32)
    suffix_length = uneven_parts(splits[13], REQUESTS, REQUESTS * SUF // 2, SUF, 1).astype(jnp.int32)
    block_slot = jax.random.permutation(splits[14], BLOCKS).astype(jnp.int32)
    return dict(queries=queries, query_gain=query_gain, new_keys=new_keys, new_values=new_values, root_keys=root_keys, root_values=root_values, branch_keys=branch_keys, branch_values=branch_values, suffix_keys=suffix_keys, suffix_values=suffix_values, out_weight=out_weight, request_branch=request_branch, branch_blocks=branch_blocks, suffix_length=suffix_length, block_slot=block_slot)


def norm_heads(raw_query, query_gain):
    mean_square = lax.optimization_barrier(jnp.mean(raw_query * raw_query, axis=-1, keepdims=True))
    return (raw_query * lax.rsqrt(mean_square + 1e-06) * query_gain.astype(jnp.float32)).astype(jnp.bfloat16)

def token_branch(branch_blocks, block_slot, slot_ids):
    block_count = block_slot.shape[0]
    block_ids = jnp.arange(block_count, dtype=jnp.int32)
    slot_block = lax.optimization_barrier(jnp.sum(jnp.where(block_slot[:, None] == slot_ids[None, :], block_ids[:, None], 0), axis=0)).astype(jnp.int32)
    cum_end = jnp.cumsum(branch_blocks).astype(jnp.int32)
    block_branch = lax.optimization_barrier(jnp.sum((cum_end[None, :] <= slot_block[:, None]).astype(jnp.int32), axis=1)).astype(jnp.int32)
    return jnp.repeat(block_branch, BLK)

def reference(queries, query_gain, new_keys, new_values, root_keys, root_values, branch_keys, branch_values, suffix_keys, suffix_values, out_weight, request_branch, branch_blocks, suffix_length, block_slot):
    score_scale = 1.0 / math.sqrt(HD)
    slot_ids = jnp.arange(BLOCKS, dtype=jnp.int32)
    shared_branch = jnp.concatenate([jnp.full((ROOT,), -1, jnp.int32), token_branch(branch_blocks, block_slot, slot_ids)])
    shared_keys = jnp.concatenate([root_keys, branch_keys], 0).astype(jnp.float32)
    shared_values = jnp.concatenate([root_values, branch_values], 0).astype(jnp.float32)
    shared_count = shared_keys.shape[0]
    own_keys = jnp.concatenate([suffix_keys, jnp.transpose(new_keys, (1, 0, 2, 3))], axis=1)
    own_values = jnp.concatenate([suffix_values, jnp.transpose(new_values, (1, 0, 2, 3))], axis=1)
    positions = jnp.arange(SUF + STEPS, dtype=jnp.int32)
    attn_steps = []
    lse_steps = []
    layer_steps = []
    for step_index in range(STEPS):
        raw_query = queries[step_index].astype(jnp.float32).reshape(REQUESTS, KVH, GROUP, HD)
        normed = norm_heads(raw_query, query_gain)

        def attend(block_item):
            query_rows, branch, keys_here, values_here, length = block_item
            query_rows = query_rows.astype(jnp.float32)
            shared_scores = jnp.einsum('hgd,thd->hgt', query_rows, shared_keys) * score_scale
            seen = (shared_branch == -1) | (shared_branch == branch)
            shared_scores = jnp.where(seen[None, None, :], shared_scores, -jnp.inf)
            own_scores = jnp.einsum('hgd,thd->hgt', query_rows, keys_here.astype(jnp.float32)) * score_scale
            own_seen = (positions < length) | (positions >= SUF) & (positions <= SUF + step_index)
            own_scores = jnp.where(own_seen[None, None, :], own_scores, -jnp.inf)
            row_top = jnp.maximum(lax.optimization_barrier(jnp.max(shared_scores, -1)), lax.optimization_barrier(jnp.max(own_scores, -1)))
            sum_exp = lax.optimization_barrier(jnp.sum(jnp.exp(shared_scores - row_top[..., None]), -1)) + lax.optimization_barrier(jnp.sum(jnp.exp(own_scores - row_top[..., None]), -1))
            log_sum = row_top + jnp.log(sum_exp)
            scores = jnp.concatenate([shared_scores, own_scores], -1)
            weights = jnp.exp(scores - log_sum[..., None]).astype(jnp.bfloat16)
            weights = lax.optimization_barrier(weights).astype(jnp.float32)
            attended = jnp.einsum('hgt,thd->hgd', weights[..., :shared_count], shared_values)
            attended = attended + jnp.einsum('hgt,thd->hgd', weights[..., shared_count:], values_here.astype(jnp.float32))
            return (attended.reshape(KVH, GROUP * HD), log_sum)
        attended, log_sum = lax.map(attend, (normed, request_branch, own_keys, own_values, suffix_length))
        attn_steps.append(attended)
        lse_steps.append(log_sum)
        attended_low = attended.astype(jnp.bfloat16)
        layer_steps.append(jnp.dot(attended_low.reshape(REQUESTS, KVH * GROUP * HD), out_weight, preferred_element_type=jnp.float32))
    return (jnp.stack(attn_steps), jnp.stack(lse_steps), jnp.stack(layer_steps))
```

```python
import functools
import math

import jax
import jax.numpy as jnp
from jax import lax
from jax.experimental import pallas as pl
from jax.experimental.pallas import tpu as pltpu
from jax.sharding import Mesh
from jax.sharding import PartitionSpec as P

HD = 128
GROUP = 16
BLK = 256
SUF = 512
STEPS = 2
OWN = 4
REQ_ROWS = STEPS * GROUP
PIECE = OWN * REQ_ROWS
STAT = 16
PACK = PIECE + STAT
NX, NZ = 4, 8
PIECES = NX * NZ
LOCAL = PIECES * OWN
SCALE = 1.0 / math.sqrt(HD)
EXP2 = SCALE * math.log2(math.e)
ITEM = 8
BATCH = 4
SLOTS = 16
VMEM = pl.BlockSpec(memory_space=pltpu.VMEM)
SMEM = pl.BlockSpec(memory_space=pltpu.SMEM)
ANY = pl.BlockSpec(memory_space=pl.ANY)
PARAMS = pltpu.CompilerParams(vmem_limit_bytes=44 * 1024 * 1024)
f32, bf16 = jnp.float32, jnp.bfloat16


def swap(a, axis, n, k):
    return lax.ppermute(a, axis, [(i, i ^ k) for i in range(n)])


def nt(a, b):
    return lax.dot_general(a, b, (((1,), (1,)), ((), ())), preferred_element_type=f32)


def nn(a, b):
    return jnp.dot(a, b, preferred_element_type=f32)


def diagonal():
    rows = lax.broadcasted_iota(jnp.int32, (PIECE, PIECE), 0)
    return rows == lax.broadcasted_iota(jnp.int32, (PIECE, PIECE), 1)


def to_lanes(column, diag):
    return jnp.sum(jnp.where(diag, column, 0.0), axis=0, keepdims=True)


def to_rows(lanes, diag):
    return jnp.sum(jnp.where(diag, lanes, 0.0), axis=1, keepdims=True)


def pack_lse(lanes):
    row = lax.broadcasted_iota(jnp.int32, (STAT, PIECE), 0)
    high = lanes.astype(bf16).astype(f32)
    middle = (lanes - high).astype(bf16).astype(f32)
    low = lanes - high - middle
    stat = jnp.where(row == 0, high, jnp.where(row == 1, middle, jnp.where(row == 2, low, 0.0)))
    return stat.astype(bf16)


def unpack_lse(stat):
    stat = stat.astype(f32)
    return stat[0:1] + stat[1:2] + stat[2:3]


def merge(parts, lses, diag):
    top = functools.reduce(jnp.maximum, lses)
    factors = [jnp.exp(lse - top) for lse in lses]
    total = functools.reduce(jnp.add, factors)
    out = 0.0
    for part, factor in zip(parts, factors):
        out = out + part() * to_rows(factor / total, diag)
    return out, top + jnp.log(total)


def norm_kernel(q_ref, gain_ref, out_ref):
    x = q_ref[...].astype(f32)
    mean_square = jnp.mean(x * x, axis=-1, keepdims=True)
    out_ref[...] = (x * lax.rsqrt(mean_square + 1e-06) * gain_ref[...]).astype(bf16)


def own_kernel(length_ref, q_ref, sk_ref, sv_ref, nk_ref, nv_ref, out_ref, lse_ref):
    q = q_ref[...]
    pad = jnp.zeros((PIECE - STEPS * OWN, HD), f32)
    new_keys = jnp.concatenate([nk_ref[...].astype(f32), pad], 0).astype(bf16)
    new_values = jnp.concatenate([nv_ref[...].astype(f32), pad], 0).astype(bf16)
    row = lax.broadcasted_iota(jnp.int32, (PIECE, PIECE), 0)
    token = lax.broadcasted_iota(jnp.int32, (PIECE, PIECE), 1)
    seen = (token < STEPS * OWN) & ((token & (OWN - 1)) == (row >> 5))
    seen = seen & ((token >> 2) <= ((row >> 4) & 1))
    new_scores = jnp.where(seen, nt(q, new_keys), -jnp.inf)
    position = lax.broadcasted_iota(jnp.int32, (REQ_ROWS, SUF), 1)
    outs, lses = [], []
    for i in range(OWN):
        rows = slice(i * REQ_ROWS, (i + 1) * REQ_ROWS)
        scores = jnp.where(position < length_ref[i], nt(q[rows], sk_ref[i]), -jnp.inf)
        fresh = new_scores[rows]
        top = jnp.maximum(
            jnp.max(scores, axis=1, keepdims=True), jnp.max(fresh, axis=1, keepdims=True)
        )
        weights = jnp.exp2((scores - top) * EXP2)
        fresh_weights = jnp.exp2((fresh - top) * EXP2)
        total = jnp.sum(weights, axis=1, keepdims=True) + jnp.sum(
            fresh_weights, axis=1, keepdims=True
        )
        out = nn(weights.astype(bf16), sv_ref[i]) + nn(fresh_weights.astype(bf16), new_values)
        outs.append(out / total)
        lses.append(top * SCALE + jnp.log(total))
    out_ref[...] = jnp.concatenate(outs, 0)
    lse = to_lanes(jnp.concatenate(lses, 0), diagonal())
    lse_ref[...] = jnp.broadcast_to(lse, lse_ref.shape)


def shared_kernel(
    meta_ref, q0, q1, q2, q3, rk0, rk1, rv0, rv1, bk0, bk1, bv0, bv1,
    out0, out1, out2, out3,
    item_block, item_part, bk, bv, q_all, acc, top_all, sum_all, part, part_top, part_sum, sems,
):
    half = bk.shape[0] // 2
    copies = []
    for n, (src, dst) in enumerate(((bk0, bk), (bk1, bk), (bv0, bv), (bv1, bv))):
        copies.append(
            pltpu.make_async_copy(src, dst.at[pl.ds((n % 2) * half, half)], sems.at[n])
        )
    for copy in copies:
        copy.start()

    def list_block(j, n):
        parts = (meta_ref[LOCAL + j] + (ITEM - 1)) >> 3

        def put(k, carry):
            item_block[n + k] = j
            item_part[n + k] = k
            return carry

        lax.fori_loop(0, parts, put, 0)
        return n + parts

    items = lax.fori_loop(0, SLOTS, list_block, 0)
    for u in range(BATCH - 1):
        item_block[items + u] = 0
        item_part[items + u] = LOCAL

    q_all[pl.ds(LOCAL * REQ_ROWS, REQ_ROWS), :] = jnp.zeros((REQ_ROWS, HD), bf16)
    acc[pl.ds(LOCAL * REQ_ROWS, REQ_ROWS), :] = jnp.zeros((REQ_ROWS, HD), f32)
    top_all[pl.ds(LOCAL * REQ_ROWS, REQ_ROWS), :] = jnp.zeros((REQ_ROWS, HD), f32)
    sum_all[pl.ds(LOCAL * REQ_ROWS, REQ_ROWS), :] = jnp.ones((REQ_ROWS, HD), f32)

    tile = 256
    quarter = NZ * PIECE
    for g, q_ref in enumerate((q0, q1, q2, q3)):

        def root_tile(t, carry):
            q = q_ref[pl.ds(pl.multiple_of(t * tile, tile), tile), :]
            rows = pl.ds(pl.multiple_of(g * quarter + t * tile, tile), tile)
            q_all[rows, :] = q
            s0 = nt(q, rk0[...])
            s1 = nt(q, rk1[...])
            top = jnp.max(jnp.maximum(s0, s1), axis=1, keepdims=True)
            w0 = jnp.exp2((s0 - top) * EXP2)
            w1 = jnp.exp2((s1 - top) * EXP2)
            total = jnp.sum(w0 + w1, axis=1, keepdims=True)
            acc[rows, :] = nn(w0.astype(bf16), rv0[...]) + nn(w1.astype(bf16), rv1[...])
            top_all[rows, :] = jnp.broadcast_to(top, (tile, HD))
            sum_all[rows, :] = jnp.broadcast_to(total, (tile, HD))
            return carry

        lax.fori_loop(0, quarter // tile, root_tile, 0, unroll=2)

    for copy in copies:
        copy.wait()

    def request_rows(block, index):
        place = meta_ref[LOCAL + SLOTS + block] + index
        found = meta_ref[jnp.minimum(place, LOCAL - 1)]
        request = jnp.where(index < meta_ref[LOCAL + block], found, LOCAL)
        return pl.ds(pl.multiple_of(request * REQ_ROWS, REQ_ROWS), REQ_ROWS)

    def batch(b, carry):
        places = []
        for u in range(BATCH):
            block = item_block[b * BATCH + u]
            first = item_part[b * BATCH + u] * ITEM
            rows = [request_rows(block, first + e) for e in range(ITEM)]
            tokens = pl.ds(pl.multiple_of(block * BLK, BLK), BLK)
            q = jnp.concatenate([q_all[r, :] for r in rows], 0)
            scores = nt(q, bk[tokens, :])
            top = jnp.max(scores, axis=1, keepdims=True)
            weights = jnp.exp2((scores - top) * EXP2)
            total = jnp.sum(weights, axis=1, keepdims=True)
            part[u] = nn(weights.astype(bf16), bv[tokens, :])
            part_top[u] = jnp.broadcast_to(top, (ITEM * REQ_ROWS, HD))
            part_sum[u] = jnp.broadcast_to(total, (ITEM * REQ_ROWS, HD))
            places.append(rows)
        for u in range(BATCH):
            rows = places[u]
            old_top = jnp.concatenate([top_all[r, :] for r in rows], 0)
            old_sum = jnp.concatenate([sum_all[r, :] for r in rows], 0)
            old_acc = jnp.concatenate([acc[r, :] for r in rows], 0)
            top = jnp.maximum(old_top, part_top[u])
            keep = jnp.exp2((old_top - top) * EXP2)
            add = jnp.exp2((part_top[u] - top) * EXP2)
            new_sum = old_sum * keep + part_sum[u] * add
            new_acc = old_acc * keep + part[u] * add
            for e, r in enumerate(rows):
                piece = slice(e * REQ_ROWS, (e + 1) * REQ_ROWS)
                top_all[r, :] = top[piece]
                sum_all[r, :] = new_sum[piece]
                acc[r, :] = new_acc[piece]
        return carry

    lax.fori_loop(0, (items + BATCH - 1) >> 2, batch, 0)

    diag = diagonal()
    for g, out in enumerate((out0, out1, out2, out3)):

        def finish(n, carry):
            rows = pl.ds(pl.multiple_of(g * quarter + n * PIECE, PIECE), PIECE)
            total = sum_all[rows, :]
            start = pl.multiple_of(n * PACK, 16)
            out[pl.ds(start, PIECE), :] = (acc[rows, :] / total).astype(bf16)
            lse = top_all[rows, :] * SCALE + jnp.log(total)
            out[pl.ds(start + PIECE, STAT), :] = pack_lse(to_lanes(lse, diag))
            return carry

        lax.fori_loop(0, NZ, finish, 0, unroll=2)


def merge_kernel(a, b, c, d, *outs):
    diag = diagonal()
    refs = (a, b, c, d)
    for n, out in enumerate(outs):
        body = slice(n * PACK, n * PACK + PIECE)
        stat = slice(n * PACK + PIECE, (n + 1) * PACK)
        merged, lse = merge(
            [lambda ref=ref: ref[body, :].astype(f32) for ref in refs],
            [unpack_lse(ref[stat, :]) for ref in refs],
            diag,
        )
        out[0:PIECE, :] = merged.astype(bf16)
        out[PIECE:PACK, :] = pack_lse(lse)


def final_kernel(*refs):
    parts, (own, own_lse, attn, attn_low, lse_out, rows) = refs[:NZ], refs[NZ:]
    diag = diagonal()
    merged, lse = merge(
        [lambda ref=ref: ref[0:PIECE, :].astype(f32) for ref in parts] + [lambda: own[...]],
        [unpack_lse(ref[PIECE:PACK, :]) for ref in parts] + [own_lse[0:1, :]],
        diag,
    )
    rows[...] = merged
    lse_out[...] = jnp.broadcast_to(lse, lse_out.shape)
    for s in range(STEPS):
        for h in range(GROUP):
            attn[s * OWN:(s + 1) * OWN, h * HD:(h + 1) * HD] = rows[
                pl.ds(s * GROUP + h, OWN, stride=REQ_ROWS), :
            ]
    attn_low[...] = attn[...].astype(bf16)


def project_kernel(where_ref, *refs):
    rows, weights, outs, terms = refs[:2 * NZ], refs[2 * NZ:2 * NZ + NX], refs[2 * NZ + NX:-1], refs[-1]
    left = jnp.concatenate([r[...].astype(f32) for r in rows], 0).astype(bf16)
    depth = left.shape[1] // 2
    for n, weight in enumerate(weights):
        low = nn(left[:, :depth], weight[...])
        high = nn(left[:, depth:], weight[...])
        columns = low.shape[1] // 2
        term = low[:, :columns] + high[:, columns:]
        count = term.shape[0] // 2
        terms[n] = jnp.concatenate([term[:count], term[count:]], 1)
    for n, out in enumerate(outs):
        out[...] = terms[where_ref[0] ^ n]


def gather_kernel(where_ref, a, b, c, d, out):
    total = a[...] + b[...] + c[...] + d[...]
    columns = out.shape[2]
    first = where_ref[1] == 0
    for n in range(NZ):
        for s in range(STEPS):
            rows = slice(n * STEPS * OWN + s * OWN, n * STEPS * OWN + (s + 1) * OWN)
            mine, other = total[rows, :columns], total[rows, columns:]
            pair = jnp.concatenate(
                [jnp.where(first, mine, other), jnp.where(first, other, mine)], 0
            )
            place = pl.multiple_of((where_ref[0] ^ n) * 2 * OWN, 2 * OWN)
            out[s, pl.ds(place, 2 * OWN), :] = pair


def plan(request_branch, branch_blocks, block_slot, x, z, core):
    leaf = (x * NZ + z) * 2 + core
    here = SLOTS // 2
    block_ids = jnp.arange(block_slot.shape[0], dtype=jnp.int32)
    offsets = jnp.arange(here, dtype=jnp.int32)
    slot_ids = jnp.concatenate([leaf * here + offsets, (leaf ^ 1) * here + offsets])
    slot_block = jnp.sum(
        jnp.where(block_slot[:, None] == slot_ids[None, :], block_ids[:, None], 0), axis=0
    )
    cum_end = jnp.cumsum(branch_blocks)
    slot_branch = jnp.sum((cum_end[None, :] <= slot_block[:, None]).astype(jnp.int32), axis=1)
    n = jnp.arange(LOCAL, dtype=jnp.int32)
    owner = ((x ^ (n >> 5)) * NZ + (z ^ ((n >> 2) & (NZ - 1)))) * 2 + core
    request = owner * OWN + (n & (OWN - 1))
    every = jnp.arange(request_branch.shape[0], dtype=jnp.int32)
    branch = jnp.sum(jnp.where(request[:, None] == every[None, :], request_branch[None, :], 0), 1)
    before = (branch[None, :] < branch[:, None]) | (
        (branch[None, :] == branch[:, None]) & (n[None, :] < n[:, None])
    )
    rank = jnp.sum(before.astype(jnp.int32), axis=1)
    ordered = jnp.sum(jnp.where(rank[:, None] == n[None, :], n[:, None], 0), axis=0)
    count = jnp.sum((slot_branch[:, None] == branch[None, :]).astype(jnp.int32), axis=1)
    start = jnp.sum((branch[None, :] < slot_branch[:, None]).astype(jnp.int32), axis=1)
    return jnp.concatenate([ordered, count, start]).astype(jnp.int32)


def struct(shape, dtype):
    return jax.ShapeDtypeStruct(shape, dtype)


def shards(
    queries,
    query_gain,
    new_keys,
    new_values,
    root_keys,
    root_values,
    branch_keys,
    branch_values,
    suffix_keys,
    suffix_values,
    out_weight,
    request_branch,
    branch_blocks,
    suffix_length,
    block_slot,
):
    kv, x, z, core = (lax.axis_index(name) for name in ("kv", "x", "z", "core"))
    raw = queries.reshape(STEPS, OWN, GROUP, HD).transpose(1, 0, 2, 3).reshape(PIECE, HD)
    normed = pl.pallas_call(
        norm_kernel, out_shape=struct((PIECE, HD), bf16), in_specs=[VMEM, VMEM], out_specs=VMEM
    )(raw, query_gain.reshape(1, HD))
    near = jnp.concatenate([normed] + [swap(normed, "z", NZ, k) for k in range(1, NZ)], 0)
    quarters = [near] + [swap(near, "x", NX, k) for k in range(1, NX)]

    shared = []
    for a in (root_keys, root_values, branch_keys, branch_values):
        flat = a.reshape(a.shape[0], HD)
        shared += [flat, swap(flat, "core", 2, 1)]
    depth = out_weight.shape[0] // 2
    folded = jnp.concatenate([out_weight[:depth], out_weight[depth:]], 1)
    weights = [folded] + [swap(folded, "x", NX, k) for k in range(1, NX)]
    meta = plan(request_branch, branch_blocks, block_slot, x, z, core)

    own, own_lse = pl.pallas_call(
        own_kernel,
        out_shape=[struct((PIECE, HD), f32), struct((8, PIECE), f32)],
        in_specs=[SMEM] + [VMEM] * 5,
        out_specs=[VMEM, VMEM],
        compiler_params=PARAMS,
    )(
        suffix_length,
        normed,
        suffix_keys.reshape(OWN, SUF, HD),
        suffix_values.reshape(OWN, SUF, HD),
        new_keys.reshape(STEPS * OWN, HD),
        new_values.reshape(STEPS * OWN, HD),
    )

    rows = LOCAL * REQ_ROWS
    spare = rows + REQ_ROWS
    branch_rows = SLOTS * BLK
    partials = pl.pallas_call(
        shared_kernel,
        out_shape=[struct((NZ * PACK, HD), bf16)] * NX,
        in_specs=[SMEM] + [VMEM] * 8 + [ANY] * 4,
        out_specs=[VMEM] * NX,
        scratch_shapes=[
            pltpu.SMEM((SLOTS * LOCAL // ITEM + BATCH,), jnp.int32),
            pltpu.SMEM((SLOTS * LOCAL // ITEM + BATCH,), jnp.int32),
            pltpu.VMEM((branch_rows, HD), bf16),
            pltpu.VMEM((branch_rows, HD), bf16),
            pltpu.VMEM((spare, HD), bf16),
            pltpu.VMEM((spare, HD), f32),
            pltpu.VMEM((spare, HD), f32),
            pltpu.VMEM((spare, HD), f32),
            pltpu.VMEM((BATCH, ITEM * REQ_ROWS, HD), f32),
            pltpu.VMEM((BATCH, ITEM * REQ_ROWS, HD), f32),
            pltpu.VMEM((BATCH, ITEM * REQ_ROWS, HD), f32),
            pltpu.SemaphoreType.DMA((4,)),
        ],
        compiler_params=PARAMS,
        cost_estimate=pl.CostEstimate(
            flops=4 * rows * HD * 2048, bytes_accessed=6 << 20, transcendentals=rows * 2048
        ),
    )(meta, *quarters, *shared)

    returned = [partials[0]] + [swap(partials[k], "x", NX, k) for k in range(1, NX)]
    merged = pl.pallas_call(
        merge_kernel,
        out_shape=[struct((PACK, HD), bf16)] * NZ,
        in_specs=[VMEM] * NX,
        out_specs=[VMEM] * NZ,
        compiler_params=PARAMS,
    )(*returned)
    landed = [merged[0]] + [swap(merged[k], "z", NZ, k) for k in range(1, NZ)]
    attn, attn_low, lse = pl.pallas_call(
        final_kernel,
        out_shape=[
            struct((STEPS * OWN, GROUP * HD), f32),
            struct((STEPS * OWN, GROUP * HD), bf16),
            struct((8, PIECE), f32),
        ],
        in_specs=[VMEM] * (NZ + 2),
        out_specs=[VMEM] * 3,
        scratch_shapes=[pltpu.VMEM((PIECE, HD), f32)],
        compiler_params=PARAMS,
    )(*landed, own, own_lse)
    attn_out = attn.reshape(STEPS, OWN, 1, GROUP * HD)
    log_total = lse[0].reshape(OWN, STEPS, GROUP).transpose(1, 0, 2).reshape(STEPS, OWN, 1, GROUP)

    held = [attn_low] + [swap(attn_low, "z", NZ, k) for k in range(1, NZ)]
    stacked = jnp.stack(held)
    across = swap(stacked, "core", 2, 1)
    columns = out_weight.shape[1]
    term = struct((NZ * STEPS * OWN, 2 * columns), f32)
    terms = pl.pallas_call(
        project_kernel,
        out_shape=[term] * NX,
        in_specs=[SMEM] + [VMEM] * (2 * NZ + NX),
        out_specs=[VMEM] * NX,
        scratch_shapes=[pltpu.VMEM((NX,) + term.shape, f32)],
        compiler_params=PARAMS,
    )((x ^ kv).reshape(1), *held, *[across[k] for k in range(NZ)], *weights)
    arrived = []
    for k in range(NX):
        pairs = [(v * NX + c, c * NX + (v ^ k)) for v in range(NX) for c in range(NX)]
        arrived.append(lax.ppermute(terms[k], ("kv", "x"), pairs))
    layer_out = pl.pallas_call(
        gather_kernel,
        out_shape=struct((STEPS, NZ * 2 * OWN, columns), f32),
        in_specs=[SMEM] + [VMEM] * NX,
        out_specs=VMEM,
        compiler_params=PARAMS,
    )(jnp.stack([z, core]), *arrived)
    return attn_out, log_total, layer_out


def solution(mesh):
    fine = Mesh(mesh.devices.reshape(4, NX, NZ, 2), ("kv", "x", "z", "core"))
    leaf = ("x", "z", "core")
    in_specs = (
        P(None, leaf, "kv", None),
        P(),
        P(None, leaf, "kv", None),
        P(None, leaf, "kv", None),
        P(leaf, "kv", None),
        P(leaf, "kv", None),
        P(leaf, "kv", None),
        P(leaf, "kv", None),
        P(leaf, None, "kv", None),
        P(leaf, None, "kv", None),
        P("kv", leaf),
        P(),
        P(),
        P(leaf),
        P(),
    )
    out_specs = (P(None, leaf, "kv", None), P(None, leaf, "kv", None), P(None, "kv", leaf))
    return jax.shard_map(shards, mesh=fine, in_specs=in_specs, out_specs=out_specs, check_vma=False)
```

```python
import functools
import math

import jax
import jax.numpy as jnp
from jax import lax
from jax.experimental import pallas as pl
from jax.experimental.pallas import tpu as pltpu
from jax.sharding import Mesh
from jax.sharding import PartitionSpec as P

HD = 128
GROUP = 16
BLK = 256
SUF = 512
STEPS = 2
OWN = 4
REQ_ROWS = STEPS * GROUP
PIECE = OWN * REQ_ROWS
STAT = 16
PACK = PIECE + STAT
NX, NZ = 4, 8
NEAR = NZ // 2
LOCAL = NX * NEAR * OWN
SCALE = 1.0 / math.sqrt(HD)
EXP2 = SCALE * math.log2(math.e)
ITEM = 4
BATCH = 8
SLOTS = 16
ROOT = 512
HELD = SLOTS // 2 * BLK
CHUNKS = 4
QUARTER = NEAR * PIECE
VMEM = pl.BlockSpec(memory_space=pltpu.VMEM)
SMEM = pl.BlockSpec(memory_space=pltpu.SMEM)
ANY = pl.BlockSpec(memory_space=pl.ANY)
PARAMS = pltpu.CompilerParams(vmem_limit_bytes=44 * 1024 * 1024)
f32, bf16 = jnp.float32, jnp.bfloat16


def swap(a, axis, n, k):
    return lax.ppermute(a, axis, [(i, i ^ k) for i in range(n)])


def nt(a, b):
    return lax.dot_general(a, b, (((1,), (1,)), ((), ())), preferred_element_type=f32)


def nn(a, b):
    return jnp.dot(a, b, preferred_element_type=f32)


def diagonal():
    rows = lax.broadcasted_iota(jnp.int32, (PIECE, PIECE), 0)
    return rows == lax.broadcasted_iota(jnp.int32, (PIECE, PIECE), 1)


def to_lanes(column, diag):
    return jnp.sum(jnp.where(diag, column, 0.0), axis=0, keepdims=True)


def to_rows(lanes, diag):
    return jnp.sum(jnp.where(diag, lanes, 0.0), axis=1, keepdims=True)


def pack_lse(lanes):
    row = lax.broadcasted_iota(jnp.int32, (STAT, PIECE), 0)
    high = lanes.astype(bf16).astype(f32)
    middle = (lanes - high).astype(bf16).astype(f32)
    low = lanes - high - middle
    stat = jnp.where(row == 0, high, jnp.where(row == 1, middle, jnp.where(row == 2, low, 0.0)))
    return stat.astype(bf16)


def unpack_lse(stat):
    stat = stat.astype(f32)
    return stat[0:1] + stat[1:2] + stat[2:3]


def merge(parts, lses, diag):
    top = functools.reduce(jnp.maximum, lses)
    factors = [jnp.exp(lse - top) for lse in lses]
    total = functools.reduce(jnp.add, factors)
    out = 0.0
    for part, factor in zip(parts, factors):
        out = out + part() * to_rows(factor / total, diag)
    return out, top + jnp.log(total)


def norm_kernel(q_ref, gain_ref, out_ref):
    x = q_ref[...].astype(f32)
    mean_square = jnp.mean(x * x, axis=-1, keepdims=True)
    out_ref[...] = (x * lax.rsqrt(mean_square + 1e-06) * gain_ref[...]).astype(bf16)


def own_kernel(length_ref, q_ref, sk_ref, sv_ref, nk_ref, nv_ref, out_ref, lse_ref):
    q = q_ref[...]
    pad = jnp.zeros((PIECE - STEPS * OWN, HD), f32)
    new_keys = jnp.concatenate([nk_ref[...].astype(f32), pad], 0).astype(bf16)
    new_values = jnp.concatenate([nv_ref[...].astype(f32), pad], 0).astype(bf16)
    row = lax.broadcasted_iota(jnp.int32, (PIECE, PIECE), 0)
    token = lax.broadcasted_iota(jnp.int32, (PIECE, PIECE), 1)
    seen = (token < STEPS * OWN) & ((token & (OWN - 1)) == (row >> 5))
    seen = seen & ((token >> 2) <= ((row >> 4) & 1))
    new_scores = jnp.where(seen, nt(q, new_keys), -jnp.inf)
    position = lax.broadcasted_iota(jnp.int32, (REQ_ROWS, SUF), 1)
    outs, lses = [], []
    for i in range(OWN):
        rows = slice(i * REQ_ROWS, (i + 1) * REQ_ROWS)
        scores = jnp.where(position < length_ref[i], nt(q[rows], sk_ref[i]), -jnp.inf)
        fresh = new_scores[rows]
        top = jnp.maximum(
            jnp.max(scores, axis=1, keepdims=True), jnp.max(fresh, axis=1, keepdims=True)
        )
        weights = jnp.exp2((scores - top) * EXP2)
        fresh_weights = jnp.exp2((fresh - top) * EXP2)
        total = jnp.sum(weights, axis=1, keepdims=True) + jnp.sum(
            fresh_weights, axis=1, keepdims=True
        )
        out = nn(weights.astype(bf16), sv_ref[i]) + nn(fresh_weights.astype(bf16), new_values)
        outs.append(out / total)
        lses.append(top * SCALE + jnp.log(total))
    out_ref[...] = jnp.concatenate(outs, 0)
    lse = to_lanes(jnp.concatenate(lses, 0), diagonal())
    lse_ref[...] = jnp.broadcast_to(lse, lse_ref.shape)


def shared_kernel(second, meta_ref, *refs):
    limbs, refs = refs[:2], refs[2:]
    if second:
        before, outs = refs[:4], refs[4:4 + NX]
        q_all, acc, top_all, sum_all = refs[4 + NX:8 + NX]
        refs = refs[8 + NX:]
    else:
        qs, roots = refs[:NX], refs[NX:NX + 2]
        q_all, acc, top_all, sum_all = refs[2 + NX:6 + NX]
        refs = refs[6 + NX:]
    item_block, item_part, held, part, part_top, part_sum, sems = refs

    copies = []
    for n in range(2):
        copies.append(
            pltpu.make_async_copy(limbs[n], held.at[pl.ds(n * 2 * HELD, 2 * HELD)], sems.at[n])
        )
    if second:
        for n, (src, dst) in enumerate(zip(before, (q_all, acc, top_all, sum_all))):
            copies.append(pltpu.make_async_copy(src, dst, sems.at[2 + n]))
    for copy in copies:
        copy.start()

    def list_block(j, n):
        parts = (meta_ref[LOCAL + j] + (ITEM - 1)) // ITEM

        def put(k, carry):
            item_block[n + k] = j
            item_part[n + k] = k
            return carry

        lax.fori_loop(0, parts, put, 0)
        return n + parts

    items = lax.fori_loop(0, SLOTS, list_block, 0)
    for u in range(BATCH - 1):
        item_block[items + u] = 0
        item_part[items + u] = LOCAL

    tile = 256
    if not second:
        spare = pl.ds(LOCAL * REQ_ROWS, REQ_ROWS)
        q_all[spare, :] = jnp.zeros((REQ_ROWS, HD), bf16)
        acc[spare, :] = jnp.zeros((REQ_ROWS, HD), f32)
        top_all[spare, :] = jnp.zeros((REQ_ROWS, HD), f32)
        sum_all[spare, :] = jnp.ones((REQ_ROWS, HD), f32)
        keys, values = [], []
        for ref in roots:
            for n in range(CHUNKS // 2):
                keys.append(ref.at[pl.ds(2 * n * ROOT, ROOT)])
                values.append(ref.at[pl.ds((2 * n + 1) * ROOT, ROOT)])
        for g, q_ref in enumerate(qs):

            def root_tile(t, carry):
                q = q_ref[pl.ds(pl.multiple_of(t * tile, tile), tile), :]
                rows = pl.ds(pl.multiple_of(g * QUARTER + t * tile, tile), tile)
                q_all[rows, :] = q
                scores = [nt(q, ref[...]) for ref in keys]
                top = jnp.max(functools.reduce(jnp.maximum, scores), axis=1, keepdims=True)
                weights = [jnp.exp2((score - top) * EXP2) for score in scores]
                total = jnp.sum(functools.reduce(jnp.add, weights), axis=1, keepdims=True)
                out = [nn(w.astype(bf16), ref[...]) for w, ref in zip(weights, values)]
                acc[rows, :] = functools.reduce(jnp.add, out)
                top_all[rows, :] = jnp.broadcast_to(top, (tile, HD))
                sum_all[rows, :] = jnp.broadcast_to(total, (tile, HD))
                return carry

            lax.fori_loop(0, QUARTER // tile, root_tile, 0, unroll=2)

    for copy in copies:
        copy.wait()

    def request_rows(block, index):
        place = meta_ref[LOCAL + SLOTS + block] + index
        found = meta_ref[jnp.minimum(place, LOCAL - 1)]
        request = jnp.where(index < meta_ref[LOCAL + block], found, LOCAL)
        return pl.ds(pl.multiple_of(request * REQ_ROWS, REQ_ROWS), REQ_ROWS)

    def batch(b, carry):
        places = []
        for u in range(BATCH):
            block = item_block[b * BATCH + u]
            first = item_part[b * BATCH + u] * ITEM
            rows = [request_rows(block, first + e) for e in range(ITEM)]
            offset = (block >> 3) * 2 * HELD + (block & 7) * BLK
            keys = held[pl.ds(pl.multiple_of(offset, BLK), BLK), :]
            values = held[pl.ds(pl.multiple_of(offset + HELD, BLK), BLK), :]
            q = jnp.concatenate([q_all[r, :] for r in rows], 0)
            scores = nt(q, keys)
            top = jnp.max(scores, axis=1, keepdims=True)
            weights = jnp.exp2((scores - top) * EXP2)
            total = jnp.sum(weights, axis=1, keepdims=True)
            part[u] = nn(weights.astype(bf16), values)
            part_top[u] = jnp.broadcast_to(top, (ITEM * REQ_ROWS, HD))
            part_sum[u] = jnp.broadcast_to(total, (ITEM * REQ_ROWS, HD))
            places.append(rows)
        for u in range(BATCH):
            rows = places[u]
            old_top = jnp.concatenate([top_all[r, :] for r in rows], 0)
            old_sum = jnp.concatenate([sum_all[r, :] for r in rows], 0)
            old_acc = jnp.concatenate([acc[r, :] for r in rows], 0)
            top = jnp.maximum(old_top, part_top[u])
            keep = jnp.exp2((old_top - top) * EXP2)
            add = jnp.exp2((part_top[u] - top) * EXP2)
            new_sum = old_sum * keep + part_sum[u] * add
            new_acc = old_acc * keep + part[u] * add
            for e, r in enumerate(rows):
                piece = slice(e * REQ_ROWS, (e + 1) * REQ_ROWS)
                top_all[r, :] = top[piece]
                sum_all[r, :] = new_sum[piece]
                acc[r, :] = new_acc[piece]
        return carry

    lax.fori_loop(0, (items + BATCH - 1) // BATCH, batch, 0)
    if not second:
        return

    diag = diagonal()
    for g, out in enumerate(outs):

        def finish(n, carry):
            rows = pl.ds(pl.multiple_of(g * QUARTER + n * PIECE, PIECE), PIECE)
            total = sum_all[rows, :]
            start = pl.multiple_of(n * PACK, 16)
            out[pl.ds(start, PIECE), :] = (acc[rows, :] / total).astype(bf16)
            lse = top_all[rows, :] * SCALE + jnp.log(total)
            out[pl.ds(start + PIECE, STAT), :] = pack_lse(to_lanes(lse, diag))
            return carry

        lax.fori_loop(0, NEAR, finish, 0, unroll=2)


def merge_kernel(a, b, c, d, *outs):
    diag = diagonal()
    refs = (a, b, c, d)
    for n, out in enumerate(outs):
        body = slice(n * PACK, n * PACK + PIECE)
        stat = slice(n * PACK + PIECE, (n + 1) * PACK)
        merged, lse = merge(
            [lambda ref=ref: ref[body, :].astype(f32) for ref in refs],
            [unpack_lse(ref[stat, :]) for ref in refs],
            diag,
        )
        out[0:PIECE, :] = merged.astype(bf16)
        out[PIECE:PACK, :] = pack_lse(lse)


def final_kernel(*refs):
    parts, (own, own_lse, attn, attn_low, lse_out, rows) = refs[:NEAR], refs[NEAR:]
    diag = diagonal()
    merged, lse = merge(
        [lambda ref=ref: ref[0:PIECE, :].astype(f32) for ref in parts] + [lambda: own[...]],
        [unpack_lse(ref[PIECE:PACK, :]) for ref in parts] + [own_lse[0:1, :]],
        diag,
    )
    rows[...] = merged
    lse_out[...] = jnp.broadcast_to(lse, lse_out.shape)
    for s in range(STEPS):
        for h in range(GROUP):
            attn[s * OWN:(s + 1) * OWN, h * HD:(h + 1) * HD] = rows[
                pl.ds(s * GROUP + h, OWN, stride=REQ_ROWS), :
            ]
    attn_low[...] = attn[...].astype(bf16)


def project_kernel(where_ref, pair_ref, here_ref, there_ref, *refs):
    weights, outs, terms = refs[:NX], refs[NX:-1], refs[-1]
    one = STEPS * OWN
    pair, here, there = [ref[...].astype(f32) for ref in (pair_ref, here_ref, there_ref)]
    first = where_ref[1] == 0
    low, high = jnp.where(first, here, there), jnp.where(first, there, here)
    left = [pair[:one]]
    other = [pair[one:]]
    for source in (low, high):
        own_side = [source[2 * n * one:(2 * n + 1) * one] for n in range(NEAR - 1)]
        other_side = [source[(2 * n + 1) * one:(2 * n + 2) * one] for n in range(NEAR - 1)]
        swapped = first if source is high else jnp.logical_not(first)
        for a, b in zip(own_side, other_side):
            left.append(jnp.where(swapped, b, a))
            other.append(jnp.where(swapped, a, b))
        if source is low:
            left.append(here[2 * (NEAR - 1) * one:])
            other.append(there[2 * (NEAR - 1) * one:])
    left = jnp.concatenate(left + other, 0).astype(bf16)
    for n, weight in enumerate(weights):
        term = nt(left, weight[...])
        count = term.shape[0] // 2
        terms[n] = jnp.concatenate([term[:count], term[count:]], 1)
    for n, out in enumerate(outs):
        out[...] = terms[where_ref[0] ^ n]


def gather_kernel(where_ref, a, b, c, d, out):
    total = a[...] + b[...] + c[...] + d[...]
    columns = out.shape[2]
    first = where_ref[1] == 0
    for n in range(NZ):
        for s in range(STEPS):
            rows = slice(n * STEPS * OWN + s * OWN, n * STEPS * OWN + (s + 1) * OWN)
            mine, other = total[rows, :columns], total[rows, columns:]
            pair = jnp.concatenate(
                [jnp.where(first, mine, other), jnp.where(first, other, mine)], 0
            )
            place = pl.multiple_of((where_ref[0] ^ n) * 2 * OWN, 2 * OWN)
            out[s, pl.ds(place, 2 * OWN), :] = pair


def plan(request_branch, branch_blocks, block_slot, x, z, core):
    leaf = (x * NZ + z) * 2 + core
    here = SLOTS // 2
    block_ids = jnp.arange(block_slot.shape[0], dtype=jnp.int32)
    j = jnp.arange(2 * SLOTS, dtype=jnp.int32)
    slot_ids = (leaf ^ (j >> 3)) * here + (j & (here - 1))
    slot_block = jnp.sum(
        jnp.where(block_slot[:, None] == slot_ids[None, :], block_ids[:, None], 0), axis=0
    )
    k = jnp.arange(branch_blocks.shape[0], dtype=jnp.int32)
    cum_end = jnp.sum(jnp.where(k[:, None] <= k[None, :], branch_blocks[:, None], 0), axis=0)
    slot_branch = jnp.sum((cum_end[None, :] <= slot_block[:, None]).astype(jnp.int32), axis=1)
    n = jnp.arange(LOCAL, dtype=jnp.int32)
    owner = ((x ^ (n >> 4)) * NZ + (z ^ (((n >> 2) & (NEAR - 1)) * 2))) * 2 + core
    request = owner * OWN + (n & (OWN - 1))
    every = jnp.arange(request_branch.shape[0], dtype=jnp.int32)
    branch = jnp.sum(jnp.where(request[:, None] == every[None, :], request_branch[None, :], 0), 1)
    before = (branch[None, :] < branch[:, None]) | (
        (branch[None, :] == branch[:, None]) & (n[None, :] < n[:, None])
    )
    rank = jnp.sum(before.astype(jnp.int32), axis=1)
    ordered = jnp.sum(jnp.where(rank[:, None] == n[None, :], n[:, None], 0), axis=0)
    count = jnp.sum((slot_branch[:, None] == branch[None, :]).astype(jnp.int32), axis=1)
    start = jnp.sum((branch[None, :] < slot_branch[:, None]).astype(jnp.int32), axis=1)
    return [
        jnp.concatenate([ordered, count[half], start[half]]).astype(jnp.int32)
        for half in (slice(0, SLOTS), slice(SLOTS, 2 * SLOTS))
    ]


def struct(shape, dtype):
    return jax.ShapeDtypeStruct(shape, dtype)


def shards(
    queries,
    query_gain,
    new_keys,
    new_values,
    root_keys,
    root_values,
    branch_keys,
    branch_values,
    suffix_keys,
    suffix_values,
    out_weight,
    request_branch,
    branch_blocks,
    suffix_length,
    block_slot,
):
    kv, x, z, core = (lax.axis_index(name) for name in ("kv", "x", "z", "core"))
    raw = queries.reshape(STEPS, OWN, GROUP, HD).transpose(1, 0, 2, 3).reshape(PIECE, HD)
    normed = pl.pallas_call(
        norm_kernel, out_shape=struct((PIECE, HD), bf16), in_specs=[VMEM, VMEM], out_specs=VMEM
    )(raw, query_gain.reshape(1, HD))
    near = jnp.concatenate([normed] + [swap(normed, "z", NZ, 2 * k) for k in range(1, NEAR)], 0)
    quarters = [near] + [swap(near, "x", NX, k) for k in range(1, NX)]

    root = jnp.concatenate([root_keys.reshape(ROOT, HD), root_values.reshape(ROOT, HD)], 0)
    limb = jnp.concatenate([branch_keys.reshape(HELD, HD), branch_values.reshape(HELD, HD)], 0)
    far = swap(limb, "z", NZ, 1)
    roots = jnp.concatenate([root, swap(root, "z", NZ, 1)], 0)
    roots = [roots, swap(roots, "core", 2, 1)]
    limbs = [limb, swap(limb, "core", 2, 1)]
    meta = plan(request_branch, branch_blocks, block_slot, x, z, core)

    rows = LOCAL * REQ_ROWS
    spare = rows + REQ_ROWS
    state = [struct((spare, HD), bf16)] + [struct((spare, HD), f32)] * 3
    most = SLOTS * LOCAL // ITEM + BATCH
    scratch = [
        pltpu.SMEM((most,), jnp.int32),
        pltpu.SMEM((most,), jnp.int32),
        pltpu.VMEM((4 * HELD, HD), bf16),
    ]
    scratch += [pltpu.VMEM((BATCH, ITEM * REQ_ROWS, HD), f32)] * 3
    scratch += [pltpu.SemaphoreType.DMA((6,))]
    cost = pl.CostEstimate(
        flops=4 * rows * HD * 2048, bytes_accessed=8 << 20, transcendentals=rows * 2048
    )
    before = pl.pallas_call(
        functools.partial(shared_kernel, False),
        out_shape=state,
        in_specs=[SMEM] + [ANY] * 2 + [VMEM] * (NX + 2),
        out_specs=[VMEM] * 4,
        scratch_shapes=scratch,
        compiler_params=PARAMS,
        cost_estimate=cost,
    )(meta[0], *limbs, *quarters, *roots)
    turned = out_weight.T
    weights = [turned] + [swap(turned, "x", NX, k) for k in range(1, NX)]
    before, weights, tied = lax.optimization_barrier((before, weights, normed))
    own, own_lse = pl.pallas_call(
        own_kernel,
        out_shape=[struct((PIECE, HD), f32), struct((8, PIECE), f32)],
        in_specs=[SMEM] + [VMEM] * 5,
        out_specs=[VMEM, VMEM],
        compiler_params=PARAMS,
    )(
        suffix_length,
        tied,
        suffix_keys.reshape(OWN, SUF, HD),
        suffix_values.reshape(OWN, SUF, HD),
        new_keys.reshape(STEPS * OWN, HD),
        new_values.reshape(STEPS * OWN, HD),
    )

    far, own, own_lse = lax.optimization_barrier((far, own, own_lse))
    far = [far, swap(far, "core", 2, 1)]
    partials = pl.pallas_call(
        functools.partial(shared_kernel, True),
        out_shape=[struct((NEAR * PACK, HD), bf16)] * NX,
        in_specs=[SMEM] + [ANY] * 6,
        out_specs=[VMEM] * NX,
        scratch_shapes=[pltpu.VMEM(part.shape, part.dtype) for part in state] + scratch,
        compiler_params=PARAMS,
        cost_estimate=cost,
    )(meta[1], *far, *before)
    returned = [partials[0]] + [swap(partials[k], "x", NX, k) for k in range(1, NX)]
    merged = pl.pallas_call(
        merge_kernel,
        out_shape=[struct((PACK, HD), bf16)] * NEAR,
        in_specs=[VMEM] * NX,
        out_specs=[VMEM] * NEAR,
        compiler_params=PARAMS,
    )(*returned)
    landed = [merged[0]] + [swap(merged[k], "z", NZ, 2 * k) for k in range(1, NEAR)]
    attn, attn_low, lse = pl.pallas_call(
        final_kernel,
        out_shape=[
            struct((STEPS * OWN, GROUP * HD), f32),
            struct((STEPS * OWN, GROUP * HD), bf16),
            struct((8, PIECE), f32),
        ],
        in_specs=[VMEM] * (NEAR + 2),
        out_specs=[VMEM] * 3,
        scratch_shapes=[pltpu.VMEM((PIECE, HD), f32)],
        compiler_params=PARAMS,
    )(*landed, own, own_lse)
    attn_out = attn.reshape(STEPS, OWN, 1, GROUP * HD)
    log_total = lse[0].reshape(OWN, STEPS, GROUP).transpose(1, 0, 2).reshape(STEPS, OWN, 1, GROUP)

    pair = jnp.concatenate([attn_low, swap(attn_low, "core", 2, 1)], 0)
    fetched = []
    for k in range(1, NEAR):
        moves = [(a * 2 + c, (a ^ (k + NEAR * c)) * 2 + c) for a in range(NZ) for c in range(2)]
        fetched.append(lax.ppermute(pair, ("z", "core"), moves))
    opposite = swap(attn_low, "z", NZ, NEAR)
    fetched = jnp.concatenate(fetched + [opposite], 0)
    rows = [pair, fetched, swap(fetched, "core", 2, 1)]
    columns = out_weight.shape[1]
    term = struct((NZ * STEPS * OWN, 2 * columns), f32)
    terms = pl.pallas_call(
        project_kernel,
        out_shape=[term] * NX,
        in_specs=[SMEM] + [VMEM] * (3 + NX),
        out_specs=[VMEM] * NX,
        scratch_shapes=[pltpu.VMEM((NX,) + term.shape, f32)],
        compiler_params=PARAMS,
    )(jnp.stack([x ^ kv, core]), *rows, *weights)
    arrived = []
    for k in range(NX):
        pairs = [(v * NX + c, c * NX + (v ^ k)) for v in range(NX) for c in range(NX)]
        arrived.append(lax.ppermute(terms[k], ("kv", "x"), pairs))
    layer_out = pl.pallas_call(
        gather_kernel,
        out_shape=struct((STEPS, NZ * 2 * OWN, columns), f32),
        in_specs=[SMEM] + [VMEM] * NX,
        out_specs=VMEM,
        compiler_params=PARAMS,
    )(jnp.stack([z, core]), *arrived)
    return attn_out, log_total, layer_out


def solution(mesh):
    fine = Mesh(mesh.devices.reshape(4, NX, NZ, 2), ("kv", "x", "z", "core"))
    leaf = ("x", "z", "core")
    in_specs = (
        P(None, leaf, "kv", None),
        P(),
        P(None, leaf, "kv", None),
        P(None, leaf, "kv", None),
        P(leaf, "kv", None),
        P(leaf, "kv", None),
        P(leaf, "kv", None),
        P(leaf, "kv", None),
        P(leaf, None, "kv", None),
        P(leaf, None, "kv", None),
        P("kv", leaf),
        P(),
        P(),
        P(leaf),
        P(),
    )
    out_specs = (P(None, leaf, "kv", None), P(None, leaf, "kv", None), P(None, "kv", leaf))
    return jax.shard_map(shards, mesh=fine, in_specs=in_specs, out_specs=out_specs, check_vma=False)
```

```python
import functools
import math

import jax
import jax.numpy as jnp
from jax import lax
from jax.experimental import pallas as pl
from jax.experimental.pallas import tpu as pltpu
from jax.sharding import Mesh
from jax.sharding import PartitionSpec as P

HD = 128
GROUP = 16
BLK = 256
SUF = 512
STEPS = 2
OWN = 4
REQ_ROWS = STEPS * GROUP
PIECE = OWN * REQ_ROWS
STAT = 16
PACK = PIECE + STAT
NX, NZ = 4, 8
NEAR = NZ // 2
LOCAL = NX * NEAR * OWN
SCALE = 1.0 / math.sqrt(HD)
EXP2 = SCALE * math.log2(math.e)
ITEM = 4
BATCH = 8
SLOTS = 8
ROOT = 512
HELD = SLOTS * BLK
CHUNKS = 4
QUARTER = NEAR * PIECE
VMEM = pl.BlockSpec(memory_space=pltpu.VMEM)
SMEM = pl.BlockSpec(memory_space=pltpu.SMEM)
ANY = pl.BlockSpec(memory_space=pl.ANY)
PARAMS = pltpu.CompilerParams(vmem_limit_bytes=44 * 1024 * 1024)
f32, bf16 = jnp.float32, jnp.bfloat16


def swap(a, axis, n, k):
    return lax.ppermute(a, axis, [(i, i ^ k) for i in range(n)])


def nt(a, b):
    return lax.dot_general(a, b, (((1,), (1,)), ((), ())), preferred_element_type=f32)


def nn(a, b):
    return jnp.dot(a, b, preferred_element_type=f32)


def diagonal():
    rows = lax.broadcasted_iota(jnp.int32, (PIECE, PIECE), 0)
    return rows == lax.broadcasted_iota(jnp.int32, (PIECE, PIECE), 1)


def to_lanes(column, diag):
    return jnp.sum(jnp.where(diag, column, 0.0), axis=0, keepdims=True)


def to_rows(lanes, diag):
    return jnp.sum(jnp.where(diag, lanes, 0.0), axis=1, keepdims=True)


def pack_lse(lanes):
    row = lax.broadcasted_iota(jnp.int32, (STAT, PIECE), 0)
    high = lanes.astype(bf16).astype(f32)
    middle = (lanes - high).astype(bf16).astype(f32)
    low = lanes - high - middle
    stat = jnp.where(row == 0, high, jnp.where(row == 1, middle, jnp.where(row == 2, low, 0.0)))
    return stat.astype(bf16)


def unpack_lse(stat):
    stat = stat.astype(f32)
    return stat[0:1] + stat[1:2] + stat[2:3]


def merge(parts, lses, diag):
    top = functools.reduce(jnp.maximum, lses)
    factors = [jnp.exp(lse - top) for lse in lses]
    total = functools.reduce(jnp.add, factors)
    out = 0.0
    for part, factor in zip(parts, factors):
        out = out + part() * to_rows(factor / total, diag)
    return out, top + jnp.log(total)


def norm_kernel(q_ref, gain_ref, out_ref, rows):
    for s in range(STEPS):
        for h in range(GROUP):
            x = q_ref[s, :, h * HD:(h + 1) * HD].astype(f32)
            rows[pl.ds(s * GROUP + h, OWN, stride=REQ_ROWS), :] = x
    x = rows[...]
    mean_square = jnp.mean(x * x, axis=-1, keepdims=True)
    out_ref[...] = (x * lax.rsqrt(mean_square + 1e-06) * gain_ref[...]).astype(bf16)


def own_kernel(length_ref, q_ref, sk_ref, sv_ref, nk_ref, nv_ref, out_ref, lse_ref):
    q = q_ref[...]
    pad = jnp.zeros((PIECE - STEPS * OWN, HD), f32)
    new_keys = jnp.concatenate([nk_ref[...].astype(f32), pad], 0).astype(bf16)
    new_values = jnp.concatenate([nv_ref[...].astype(f32), pad], 0).astype(bf16)
    row = lax.broadcasted_iota(jnp.int32, (PIECE, PIECE), 0)
    token = lax.broadcasted_iota(jnp.int32, (PIECE, PIECE), 1)
    seen = (token < STEPS * OWN) & ((token & (OWN - 1)) == (row >> 5))
    seen = seen & ((token >> 2) <= ((row >> 4) & 1))
    new_scores = jnp.where(seen, nt(q, new_keys), -jnp.inf)
    position = lax.broadcasted_iota(jnp.int32, (REQ_ROWS, SUF), 1)
    outs, lses = [], []
    for i in range(OWN):
        rows = slice(i * REQ_ROWS, (i + 1) * REQ_ROWS)
        scores = jnp.where(position < length_ref[i], nt(q[rows], sk_ref[i]), -jnp.inf)
        fresh = new_scores[rows]
        top = jnp.maximum(
            jnp.max(scores, axis=1, keepdims=True), jnp.max(fresh, axis=1, keepdims=True)
        )
        weights = jnp.exp2((scores - top) * EXP2)
        fresh_weights = jnp.exp2((fresh - top) * EXP2)
        total = jnp.sum(weights, axis=1, keepdims=True) + jnp.sum(
            fresh_weights, axis=1, keepdims=True
        )
        out = nn(weights.astype(bf16), sv_ref[i]) + nn(fresh_weights.astype(bf16), new_values)
        outs.append(out / total)
        lses.append(top * SCALE + jnp.log(total))
    out_ref[...] = jnp.concatenate(outs, 0)
    lse = to_lanes(jnp.concatenate(lses, 0), diagonal())
    lse_ref[...] = jnp.broadcast_to(lse, lse_ref.shape)


def shared_kernel(second, meta_ref, *refs):
    count = CHUNKS - 1 if second else 1
    slots = count * SLOTS
    limbs, refs = refs[:count], refs[count:]
    if second:
        before, outs = refs[:4], refs[4:4 + NX]
        q_all, acc, top_all, sum_all = refs[4 + NX:8 + NX]
        refs = refs[8 + NX:]
    else:
        qs, roots = refs[:NX], refs[NX:NX + CHUNKS]
        q_all, acc, top_all, sum_all = refs[NX + CHUNKS:NX + CHUNKS + 4]
        refs = refs[NX + CHUNKS + 4:]
    item_block, item_part, held, part, part_top, part_sum, sems = refs

    copies = []
    for n in range(count):
        copies.append(
            pltpu.make_async_copy(limbs[n], held.at[pl.ds(n * 2 * HELD, 2 * HELD)], sems.at[n])
        )
    if second:
        for n, (src, dst) in enumerate(zip(before, (q_all, acc, top_all, sum_all))):
            copies.append(pltpu.make_async_copy(src, dst, sems.at[count + n]))
    for copy in copies:
        copy.start()

    def list_block(j, n):
        parts = (meta_ref[LOCAL + j] + (ITEM - 1)) // ITEM

        def put(k, carry):
            item_block[n + k] = j
            item_part[n + k] = k
            return carry

        lax.fori_loop(0, parts, put, 0)
        return n + parts

    items = lax.fori_loop(0, slots, list_block, 0)
    for u in range(BATCH - 1):
        item_block[items + u] = 0
        item_part[items + u] = LOCAL

    tile = 256
    if not second:
        spare = pl.ds(LOCAL * REQ_ROWS, REQ_ROWS)
        q_all[spare, :] = jnp.zeros((REQ_ROWS, HD), bf16)
        acc[spare, :] = jnp.zeros((REQ_ROWS, HD), f32)
        top_all[spare, :] = jnp.zeros((REQ_ROWS, HD), f32)
        sum_all[spare, :] = jnp.ones((REQ_ROWS, HD), f32)
        keys = [ref.at[pl.ds(0, ROOT)] for ref in roots]
        values = [ref.at[pl.ds(ROOT, ROOT)] for ref in roots]
        for g, q_ref in enumerate(qs):

            def root_tile(t, carry):
                q = q_ref[pl.ds(pl.multiple_of(t * tile, tile), tile), :]
                rows = pl.ds(pl.multiple_of(g * QUARTER + t * tile, tile), tile)
                q_all[rows, :] = q
                scores = [nt(q, ref[...]) for ref in keys]
                top = jnp.max(functools.reduce(jnp.maximum, scores), axis=1, keepdims=True)
                weights = [jnp.exp2((score - top) * EXP2) for score in scores]
                total = jnp.sum(functools.reduce(jnp.add, weights), axis=1, keepdims=True)
                out = [nn(w.astype(bf16), ref[...]) for w, ref in zip(weights, values)]
                acc[rows, :] = functools.reduce(jnp.add, out)
                top_all[rows, :] = jnp.broadcast_to(top, (tile, HD))
                sum_all[rows, :] = jnp.broadcast_to(total, (tile, HD))
                return carry

            lax.fori_loop(0, QUARTER // tile, root_tile, 0, unroll=2)

    for copy in copies:
        copy.wait()

    def request_rows(block, index):
        place = meta_ref[LOCAL + slots + block] + index
        found = meta_ref[jnp.minimum(place, LOCAL - 1)]
        request = jnp.where(index < meta_ref[LOCAL + block], found, LOCAL)
        return pl.ds(pl.multiple_of(request * REQ_ROWS, REQ_ROWS), REQ_ROWS)

    def batch(b, carry):
        places = []
        for u in range(BATCH):
            block = item_block[b * BATCH + u]
            first = item_part[b * BATCH + u] * ITEM
            rows = [request_rows(block, first + e) for e in range(ITEM)]
            offset = (block >> 3) * 2 * HELD + (block & 7) * BLK
            keys = held[pl.ds(pl.multiple_of(offset, BLK), BLK), :]
            values = held[pl.ds(pl.multiple_of(offset + HELD, BLK), BLK), :]
            q = jnp.concatenate([q_all[r, :] for r in rows], 0)
            scores = nt(q, keys)
            top = jnp.max(scores, axis=1, keepdims=True)
            weights = jnp.exp2((scores - top) * EXP2)
            total = jnp.sum(weights, axis=1, keepdims=True)
            part[u] = nn(weights.astype(bf16), values)
            part_top[u] = jnp.broadcast_to(top, (ITEM * REQ_ROWS, HD))
            part_sum[u] = jnp.broadcast_to(total, (ITEM * REQ_ROWS, HD))
            places.append(rows)
        for u in range(BATCH):
            rows = places[u]
            old_top = jnp.concatenate([top_all[r, :] for r in rows], 0)
            old_sum = jnp.concatenate([sum_all[r, :] for r in rows], 0)
            old_acc = jnp.concatenate([acc[r, :] for r in rows], 0)
            top = jnp.maximum(old_top, part_top[u])
            keep = jnp.exp2((old_top - top) * EXP2)
            add = jnp.exp2((part_top[u] - top) * EXP2)
            new_sum = old_sum * keep + part_sum[u] * add
            new_acc = old_acc * keep + part[u] * add
            for e, r in enumerate(rows):
                piece = slice(e * REQ_ROWS, (e + 1) * REQ_ROWS)
                top_all[r, :] = top[piece]
                sum_all[r, :] = new_sum[piece]
                acc[r, :] = new_acc[piece]
        return carry

    lax.fori_loop(0, (items + BATCH - 1) // BATCH, batch, 0)
    if not second:
        return

    diag = diagonal()
    for g, out in enumerate(outs):

        def finish(n, carry):
            rows = pl.ds(pl.multiple_of(g * QUARTER + n * PIECE, PIECE), PIECE)
            total = sum_all[rows, :]
            start = pl.multiple_of(n * PACK, 16)
            out[pl.ds(start, PIECE), :] = (acc[rows, :] / total).astype(bf16)
            lse = top_all[rows, :] * SCALE + jnp.log(total)
            out[pl.ds(start + PIECE, STAT), :] = pack_lse(to_lanes(lse, diag))
            return carry

        lax.fori_loop(0, NEAR, finish, 0, unroll=2)


def merge_kernel(a, b, c, d, *outs):
    diag = diagonal()
    refs = (a, b, c, d)
    for n, out in enumerate(outs):
        body = slice(n * PACK, n * PACK + PIECE)
        stat = slice(n * PACK + PIECE, (n + 1) * PACK)
        merged, lse = merge(
            [lambda ref=ref: ref[body, :].astype(f32) for ref in refs],
            [unpack_lse(ref[stat, :]) for ref in refs],
            diag,
        )
        out[0:PIECE, :] = merged.astype(bf16)
        out[PIECE:PACK, :] = pack_lse(lse)


def final_kernel(*refs):
    parts, (own, own_lse, attn, attn_low, lse_out, rows) = refs[:NEAR], refs[NEAR:]
    diag = diagonal()
    merged, lse = merge(
        [lambda ref=ref: ref[0:PIECE, :].astype(f32) for ref in parts] + [lambda: own[...]],
        [unpack_lse(ref[PIECE:PACK, :]) for ref in parts] + [own_lse[0:1, :]],
        diag,
    )
    rows[...] = merged
    lse_out[...] = jnp.broadcast_to(lse, lse_out.shape)
    for s in range(STEPS):
        for h in range(GROUP):
            attn[s * OWN:(s + 1) * OWN, h * HD:(h + 1) * HD] = rows[
                pl.ds(s * GROUP + h, OWN, stride=REQ_ROWS), :
            ]
    attn_low[...] = attn[...].astype(bf16)


def project_kernel(where_ref, pair_ref, here_ref, there_ref, *refs):
    weights, outs, terms = refs[:NX], refs[NX:-1], refs[-1]
    one = STEPS * OWN
    pair, here, there = [ref[...].astype(f32) for ref in (pair_ref, here_ref, there_ref)]
    first = where_ref[1] == 0
    low, high = jnp.where(first, here, there), jnp.where(first, there, here)
    left = [pair[:one]]
    other = [pair[one:]]
    for source in (low, high):
        own_side = [source[2 * n * one:(2 * n + 1) * one] for n in range(NEAR - 1)]
        other_side = [source[(2 * n + 1) * one:(2 * n + 2) * one] for n in range(NEAR - 1)]
        swapped = first if source is high else jnp.logical_not(first)
        for a, b in zip(own_side, other_side):
            left.append(jnp.where(swapped, b, a))
            other.append(jnp.where(swapped, a, b))
        if source is low:
            left.append(here[2 * (NEAR - 1) * one:])
            other.append(there[2 * (NEAR - 1) * one:])
    left = jnp.concatenate(left + other, 0).astype(bf16)
    for n, weight in enumerate(weights):
        term = nt(left, weight[...])
        count = term.shape[0] // 2
        terms[n] = jnp.concatenate([term[:count], term[count:]], 1)
    for n, out in enumerate(outs):
        out[...] = terms[where_ref[0] ^ n]


def gather_kernel(where_ref, a, b, c, d, out):
    total = a[...] + b[...] + c[...] + d[...]
    columns = out.shape[2]
    first = where_ref[1] == 0
    for n in range(NZ):
        for s in range(STEPS):
            rows = slice(n * STEPS * OWN + s * OWN, n * STEPS * OWN + (s + 1) * OWN)
            mine, other = total[rows, :columns], total[rows, columns:]
            pair = jnp.concatenate(
                [jnp.where(first, mine, other), jnp.where(first, other, mine)], 0
            )
            place = pl.multiple_of((where_ref[0] ^ n) * 2 * OWN, 2 * OWN)
            out[s, pl.ds(place, 2 * OWN), :] = pair


def plan(request_branch, branch_blocks, block_slot, x, z, core):
    leaf = (x * NZ + z) * 2 + core
    here = SLOTS
    block_ids = jnp.arange(block_slot.shape[0], dtype=jnp.int32)
    j = jnp.arange(CHUNKS * SLOTS, dtype=jnp.int32)
    slot_ids = (leaf ^ (j >> 3)) * here + (j & (here - 1))
    slot_block = jnp.sum(
        jnp.where(block_slot[:, None] == slot_ids[None, :], block_ids[:, None], 0), axis=0
    )
    k = jnp.arange(branch_blocks.shape[0], dtype=jnp.int32)
    cum_end = jnp.sum(jnp.where(k[:, None] <= k[None, :], branch_blocks[:, None], 0), axis=0)
    slot_branch = jnp.sum((cum_end[None, :] <= slot_block[:, None]).astype(jnp.int32), axis=1)
    n = jnp.arange(LOCAL, dtype=jnp.int32)
    owner = ((x ^ (n >> 4)) * NZ + (z ^ (((n >> 2) & (NEAR - 1)) * 2))) * 2 + core
    request = owner * OWN + (n & (OWN - 1))
    every = jnp.arange(request_branch.shape[0], dtype=jnp.int32)
    branch = jnp.sum(jnp.where(request[:, None] == every[None, :], request_branch[None, :], 0), 1)
    before = (branch[None, :] < branch[:, None]) | (
        (branch[None, :] == branch[:, None]) & (n[None, :] < n[:, None])
    )
    rank = jnp.sum(before.astype(jnp.int32), axis=1)
    ordered = jnp.sum(jnp.where(rank[:, None] == n[None, :], n[:, None], 0), axis=0)
    count = jnp.sum((slot_branch[:, None] == branch[None, :]).astype(jnp.int32), axis=1)
    start = jnp.sum((branch[None, :] < slot_branch[:, None]).astype(jnp.int32), axis=1)
    return [
        jnp.concatenate([ordered, count[half], start[half]]).astype(jnp.int32)
        for half in (slice(0, SLOTS), slice(SLOTS, CHUNKS * SLOTS))
    ]


def struct(shape, dtype):
    return jax.ShapeDtypeStruct(shape, dtype)


def shards(
    queries,
    query_gain,
    new_keys,
    new_values,
    root_keys,
    root_values,
    branch_keys,
    branch_values,
    suffix_keys,
    suffix_values,
    out_weight,
    request_branch,
    branch_blocks,
    suffix_length,
    block_slot,
):
    kv, x, z, core = (lax.axis_index(name) for name in ("kv", "x", "z", "core"))
    normed = pl.pallas_call(
        norm_kernel,
        out_shape=struct((PIECE, HD), bf16),
        in_specs=[VMEM, VMEM],
        out_specs=VMEM,
        scratch_shapes=[pltpu.VMEM((PIECE, HD), f32)],
    )(queries.reshape(STEPS, OWN, GROUP * HD), query_gain.reshape(1, HD))
    root = jnp.concatenate([root_keys.reshape(ROOT, HD), root_values.reshape(ROOT, HD)], 0)
    limb = jnp.concatenate([branch_keys.reshape(HELD, HD), branch_values.reshape(HELD, HD)], 0)
    side_root, limb = lax.optimization_barrier((swap(root, "core", 2, 1), limb))
    far_root, far = swap(root, "z", NZ, 1), swap(limb, "z", NZ, 1)
    near = jnp.concatenate([normed] + [swap(normed, "z", NZ, 2 * k) for k in range(1, NEAR)], 0)
    quarters = [near] + [swap(near, "x", NX, k) for k in range(1, NX)]

    roots = [root, far_root, side_root, swap(far_root, "core", 2, 1)]
    quarters[2], side = lax.optimization_barrier((quarters[2], limb))
    side = swap(side, "core", 2, 1)
    meta = plan(request_branch, branch_blocks, block_slot, x, z, core)

    rows = LOCAL * REQ_ROWS
    spare = rows + REQ_ROWS
    state = [struct((spare, HD), bf16)] + [struct((spare, HD), f32)] * 3

    def scratch(count):
        most = count * SLOTS * LOCAL // ITEM + BATCH
        lists = [pltpu.SMEM((most,), jnp.int32)] * 2
        parts = [pltpu.VMEM((BATCH, ITEM * REQ_ROWS, HD), f32)] * 3
        held = [pltpu.VMEM((count * 2 * HELD, HD), bf16)]
        return lists + held + parts + [pltpu.SemaphoreType.DMA((CHUNKS + 3,))]

    cost = pl.CostEstimate(
        flops=4 * rows * HD * 2048, bytes_accessed=8 << 20, transcendentals=rows * 2048
    )
    before = pl.pallas_call(
        functools.partial(shared_kernel, False),
        out_shape=state,
        in_specs=[SMEM] + [ANY] + [VMEM] * (NX + CHUNKS),
        out_specs=[VMEM] * 4,
        scratch_shapes=scratch(1),
        compiler_params=PARAMS,
        cost_estimate=cost,
    )(meta[0], limb, *quarters, *roots)
    turned = out_weight.T
    weights = [turned] + [swap(turned, "x", NX, k) for k in range(1, NX)]
    before, weights, tied = lax.optimization_barrier((before, weights, normed))
    own, own_lse = pl.pallas_call(
        own_kernel,
        out_shape=[struct((PIECE, HD), f32), struct((8, PIECE), f32)],
        in_specs=[SMEM] + [VMEM] * 5,
        out_specs=[VMEM, VMEM],
        compiler_params=PARAMS,
    )(
        suffix_length,
        tied,
        suffix_keys.reshape(OWN, SUF, HD),
        suffix_values.reshape(OWN, SUF, HD),
        new_keys.reshape(STEPS * OWN, HD),
        new_values.reshape(STEPS * OWN, HD),
    )

    far, own, own_lse = lax.optimization_barrier((far, own, own_lse))
    limbs = [side, far, swap(far, "core", 2, 1)]
    partials = pl.pallas_call(
        functools.partial(shared_kernel, True),
        out_shape=[struct((NEAR * PACK, HD), bf16)] * NX,
        in_specs=[SMEM] + [ANY] * (CHUNKS + 3),
        out_specs=[VMEM] * NX,
        scratch_shapes=[pltpu.VMEM(part.shape, part.dtype) for part in state] + scratch(CHUNKS - 1),
        compiler_params=PARAMS,
        cost_estimate=cost,
    )(meta[1], *limbs, *before)
    returned = [partials[0]] + [swap(partials[k], "x", NX, k) for k in range(1, NX)]
    merged = pl.pallas_call(
        merge_kernel,
        out_shape=[struct((PACK, HD), bf16)] * NEAR,
        in_specs=[VMEM] * NX,
        out_specs=[VMEM] * NEAR,
        compiler_params=PARAMS,
    )(*returned)
    landed = [merged[0]] + [swap(merged[k], "z", NZ, 2 * k) for k in range(1, NEAR)]
    attn, attn_low, lse = pl.pallas_call(
        final_kernel,
        out_shape=[
            struct((STEPS * OWN, GROUP * HD), f32),
            struct((STEPS * OWN, GROUP * HD), bf16),
            struct((8, PIECE), f32),
        ],
        in_specs=[VMEM] * (NEAR + 2),
        out_specs=[VMEM] * 3,
        scratch_shapes=[pltpu.VMEM((PIECE, HD), f32)],
        compiler_params=PARAMS,
    )(*landed, own, own_lse)
    attn_out = attn.reshape(STEPS, OWN, 1, GROUP * HD)
    log_total = lse[0].reshape(OWN, STEPS, GROUP).transpose(1, 0, 2).reshape(STEPS, OWN, 1, GROUP)

    pair = jnp.concatenate([attn_low, swap(attn_low, "core", 2, 1)], 0)
    fetched = []
    for k in range(1, NEAR):
        moves = [(a * 2 + c, (a ^ (k + NEAR * c)) * 2 + c) for a in range(NZ) for c in range(2)]
        fetched.append(lax.ppermute(pair, ("z", "core"), moves))
    opposite = swap(attn_low, "z", NZ, NEAR)
    fetched = jnp.concatenate(fetched + [opposite], 0)
    rows = [pair, fetched, swap(fetched, "core", 2, 1)]
    columns = out_weight.shape[1]
    term = struct((NZ * STEPS * OWN, 2 * columns), f32)
    terms = pl.pallas_call(
        project_kernel,
        out_shape=[term] * NX,
        in_specs=[SMEM] + [VMEM] * (3 + NX),
        out_specs=[VMEM] * NX,
        scratch_shapes=[pltpu.VMEM((NX,) + term.shape, f32)],
        compiler_params=PARAMS,
    )(jnp.stack([x ^ kv, core]), *rows, *weights)
    arrived = []
    for k in range(NX):
        pairs = [(v * NX + c, c * NX + (v ^ k)) for v in range(NX) for c in range(NX)]
        arrived.append(lax.ppermute(terms[k], ("kv", "x"), pairs))
    layer_out = pl.pallas_call(
        gather_kernel,
        out_shape=struct((STEPS, NZ * 2 * OWN, columns), f32),
        in_specs=[SMEM] + [VMEM] * NX,
        out_specs=VMEM,
        compiler_params=PARAMS,
    )(jnp.stack([z, core]), *arrived)
    return attn_out, log_total, layer_out


def solution(mesh):
    fine = Mesh(mesh.devices.reshape(4, NX, NZ, 2), ("kv", "x", "z", "core"))
    leaf = ("x", "z", "core")
    in_specs = (
        P(None, leaf, "kv", None),
        P(),
        P(None, leaf, "kv", None),
        P(None, leaf, "kv", None),
        P(leaf, "kv", None),
        P(leaf, "kv", None),
        P(leaf, "kv", None),
        P(leaf, "kv", None),
        P(leaf, None, "kv", None),
        P(leaf, None, "kv", None),
        P("kv", leaf),
        P(),
        P(),
        P(leaf),
        P(),
    )
    out_specs = (P(None, leaf, "kv", None), P(None, leaf, "kv", None), P(None, "kv", leaf))
    return jax.shard_map(shards, mesh=fine, in_specs=in_specs, out_specs=out_specs, check_vma=False)
```

```python
import functools
import math

import jax
import jax.numpy as jnp
from jax import lax
from jax.experimental import pallas as pl
from jax.experimental.pallas import tpu as pltpu
from jax.sharding import Mesh
from jax.sharding import PartitionSpec as P

HD = 128
GROUP = 16
BLK = 256
SUF = 512
STEPS = 2
OWN = 4
REQ_ROWS = STEPS * GROUP
PIECE = OWN * REQ_ROWS
STAT = 16
PACK = PIECE + STAT
NX, NZ = 4, 8
NEAR = NZ // 2
LOCAL = NX * NEAR * OWN
SCALE = 1.0 / math.sqrt(HD)
EXP2 = SCALE * math.log2(math.e)
ITEM = 4
BATCH = 16
SLOTS = 8
ROOT = 512
HELD = SLOTS * BLK
CHUNKS = 4
QUARTER = NEAR * PIECE
VMEM = pl.BlockSpec(memory_space=pltpu.VMEM)
SMEM = pl.BlockSpec(memory_space=pltpu.SMEM)
ANY = pl.BlockSpec(memory_space=pl.ANY)
PARAMS = pltpu.CompilerParams(vmem_limit_bytes=44 * 1024 * 1024)
f32, bf16 = jnp.float32, jnp.bfloat16


def swap(a, axis, n, k):
    return lax.ppermute(a, axis, [(i, i ^ k) for i in range(n)])


def nt(a, b):
    return lax.dot_general(a, b, (((1,), (1,)), ((), ())), preferred_element_type=f32)


def nn(a, b):
    return jnp.dot(a, b, preferred_element_type=f32)


def diagonal():
    rows = lax.broadcasted_iota(jnp.int32, (PIECE, PIECE), 0)
    return rows == lax.broadcasted_iota(jnp.int32, (PIECE, PIECE), 1)


def to_lanes(column, diag):
    return jnp.sum(jnp.where(diag, column, 0.0), axis=0, keepdims=True)


def to_rows(lanes, diag):
    return jnp.sum(jnp.where(diag, lanes, 0.0), axis=1, keepdims=True)


def pack_lse(lanes):
    row = lax.broadcasted_iota(jnp.int32, (STAT, PIECE), 0)
    high = lanes.astype(bf16).astype(f32)
    middle = (lanes - high).astype(bf16).astype(f32)
    low = lanes - high - middle
    stat = jnp.where(row == 0, high, jnp.where(row == 1, middle, jnp.where(row == 2, low, 0.0)))
    return stat.astype(bf16)


def unpack_lse(stat):
    stat = stat.astype(f32)
    return stat[0:1] + stat[1:2] + stat[2:3]


def merge(parts, lses, diag):
    top = functools.reduce(jnp.maximum, lses)
    factors = [jnp.exp(lse - top) for lse in lses]
    total = functools.reduce(jnp.add, factors)
    out = 0.0
    for part, factor in zip(parts, factors):
        out = out + part() * to_rows(factor / total, diag)
    return out, top + jnp.log(total)


def norm_kernel(q_ref, gain_ref, out_ref, rows):
    for s in range(STEPS):
        for h in range(GROUP):
            x = q_ref[s, :, h * HD:(h + 1) * HD].astype(f32)
            rows[pl.ds(s * GROUP + h, OWN, stride=REQ_ROWS), :] = x
    x = rows[...]
    mean_square = jnp.mean(x * x, axis=-1, keepdims=True)
    out_ref[...] = (x * lax.rsqrt(mean_square + 1e-06) * gain_ref[...]).astype(bf16)


def own_kernel(length_ref, q_ref, sk_ref, sv_ref, nk_ref, nv_ref, out_ref, lse_ref):
    q = q_ref[...]
    pad = jnp.zeros((PIECE - STEPS * OWN, HD), f32)
    new_keys = jnp.concatenate([nk_ref[...].astype(f32), pad], 0).astype(bf16)
    new_values = jnp.concatenate([nv_ref[...].astype(f32), pad], 0).astype(bf16)
    row = lax.broadcasted_iota(jnp.int32, (PIECE, PIECE), 0)
    token = lax.broadcasted_iota(jnp.int32, (PIECE, PIECE), 1)
    seen = (token < STEPS * OWN) & ((token & (OWN - 1)) == (row >> 5))
    seen = seen & ((token >> 2) <= ((row >> 4) & 1))
    new_scores = jnp.where(seen, nt(q, new_keys), -jnp.inf)
    position = lax.broadcasted_iota(jnp.int32, (REQ_ROWS, SUF), 1)
    outs, lses = [], []
    for i in range(OWN):
        rows = slice(i * REQ_ROWS, (i + 1) * REQ_ROWS)
        scores = jnp.where(position < length_ref[i], nt(q[rows], sk_ref[i]), -jnp.inf)
        fresh = new_scores[rows]
        top = jnp.maximum(
            jnp.max(scores, axis=1, keepdims=True), jnp.max(fresh, axis=1, keepdims=True)
        )
        weights = jnp.exp2((scores - top) * EXP2)
        fresh_weights = jnp.exp2((fresh - top) * EXP2)
        total = jnp.sum(weights, axis=1, keepdims=True) + jnp.sum(
            fresh_weights, axis=1, keepdims=True
        )
        out = nn(weights.astype(bf16), sv_ref[i]) + nn(fresh_weights.astype(bf16), new_values)
        outs.append(out / total)
        lses.append(top * SCALE + jnp.log(total))
    out_ref[...] = jnp.concatenate(outs, 0)
    lse = to_lanes(jnp.concatenate(lses, 0), diagonal())
    lse_ref[...] = jnp.broadcast_to(lse, lse_ref.shape)


def shared_kernel(second, meta_ref, *refs):
    count = CHUNKS - 1 if second else 1
    slots = count * SLOTS
    limbs, refs = refs[:count], refs[count:]
    if second:
        before, outs = refs[:4], refs[4:4 + NX]
        q_all, acc, top_all, sum_all = refs[4 + NX:8 + NX]
        refs = refs[8 + NX:]
    else:
        qs, roots = refs[:NX], refs[NX:NX + CHUNKS]
        q_all, acc, top_all, sum_all = refs[NX + CHUNKS:NX + CHUNKS + 4]
        refs = refs[NX + CHUNKS + 4:]
    item_block, item_part, held, part, part_top, part_sum, sems = refs

    copies = []
    for n in range(count):
        copies.append(
            pltpu.make_async_copy(limbs[n], held.at[pl.ds(n * 2 * HELD, 2 * HELD)], sems.at[n])
        )
    if second:
        for n, (src, dst) in enumerate(zip(before, (q_all, acc, top_all, sum_all))):
            copies.append(pltpu.make_async_copy(src, dst, sems.at[count + n]))
    for copy in copies:
        copy.start()

    def list_block(j, n):
        parts = (meta_ref[LOCAL + j] + (ITEM - 1)) // ITEM

        def put(k, carry):
            item_block[n + k] = j
            item_part[n + k] = k
            return carry

        lax.fori_loop(0, parts, put, 0)
        return n + parts

    items = lax.fori_loop(0, slots, list_block, 0)
    for u in range(BATCH - 1):
        item_block[items + u] = 0
        item_part[items + u] = LOCAL

    tile = 256
    if not second:
        spare = pl.ds(LOCAL * REQ_ROWS, REQ_ROWS)
        q_all[spare, :] = jnp.zeros((REQ_ROWS, HD), bf16)
        acc[spare, :] = jnp.zeros((REQ_ROWS, HD), f32)
        top_all[spare, :] = jnp.zeros((REQ_ROWS, HD), f32)
        sum_all[spare, :] = jnp.ones((REQ_ROWS, HD), f32)
        keys = [ref.at[pl.ds(0, ROOT)] for ref in roots]
        values = [ref.at[pl.ds(ROOT, ROOT)] for ref in roots]
        for g, q_ref in enumerate(qs):

            def root_tile(t, carry):
                q = q_ref[pl.ds(pl.multiple_of(t * tile, tile), tile), :]
                rows = pl.ds(pl.multiple_of(g * QUARTER + t * tile, tile), tile)
                q_all[rows, :] = q
                scores = [nt(q, ref[...]) for ref in keys]
                top = jnp.max(functools.reduce(jnp.maximum, scores), axis=1, keepdims=True)
                weights = [jnp.exp2((score - top) * EXP2) for score in scores]
                total = jnp.sum(functools.reduce(jnp.add, weights), axis=1, keepdims=True)
                out = [nn(w.astype(bf16), ref[...]) for w, ref in zip(weights, values)]
                acc[rows, :] = functools.reduce(jnp.add, out)
                top_all[rows, :] = jnp.broadcast_to(top, (tile, HD))
                sum_all[rows, :] = jnp.broadcast_to(total, (tile, HD))
                return carry

            lax.fori_loop(0, QUARTER // tile, root_tile, 0, unroll=2)

    for copy in copies:
        copy.wait()

    def request_rows(block, index):
        place = meta_ref[LOCAL + slots + block] + index
        found = meta_ref[jnp.minimum(place, LOCAL - 1)]
        request = jnp.where(index < meta_ref[LOCAL + block], found, LOCAL)
        return pl.ds(pl.multiple_of(request * REQ_ROWS, REQ_ROWS), REQ_ROWS)

    def batch(b, carry):
        places = []
        for u in range(BATCH):
            block = item_block[b * BATCH + u]
            first = item_part[b * BATCH + u] * ITEM
            rows = [request_rows(block, first + e) for e in range(ITEM)]
            offset = (block >> 3) * 2 * HELD + (block & 7) * BLK
            keys = held[pl.ds(pl.multiple_of(offset, BLK), BLK), :]
            values = held[pl.ds(pl.multiple_of(offset + HELD, BLK), BLK), :]
            q = jnp.concatenate([q_all[r, :] for r in rows], 0)
            scores = nt(q, keys)
            top = jnp.max(scores, axis=1, keepdims=True)
            weights = jnp.exp2((scores - top) * EXP2)
            total = jnp.sum(weights, axis=1, keepdims=True)
            part[u] = nn(weights.astype(bf16), values)
            part_top[u] = jnp.broadcast_to(top, (ITEM * REQ_ROWS, HD))
            part_sum[u] = jnp.broadcast_to(total, (ITEM * REQ_ROWS, HD))
            places.append(rows)
        for u in range(BATCH):
            rows = places[u]
            old_top = jnp.concatenate([top_all[r, :] for r in rows], 0)
            old_sum = jnp.concatenate([sum_all[r, :] for r in rows], 0)
            old_acc = jnp.concatenate([acc[r, :] for r in rows], 0)
            top = jnp.maximum(old_top, part_top[u])
            keep = jnp.exp2((old_top - top) * EXP2)
            add = jnp.exp2((part_top[u] - top) * EXP2)
            new_sum = old_sum * keep + part_sum[u] * add
            new_acc = old_acc * keep + part[u] * add
            for e, r in enumerate(rows):
                piece = slice(e * REQ_ROWS, (e + 1) * REQ_ROWS)
                top_all[r, :] = top[piece]
                sum_all[r, :] = new_sum[piece]
                acc[r, :] = new_acc[piece]
        return carry

    lax.fori_loop(0, (items + BATCH - 1) // BATCH, batch, 0)
    if not second:
        return

    diag = diagonal()
    for g, out in enumerate(outs):

        def finish(n, carry):
            rows = pl.ds(pl.multiple_of(g * QUARTER + n * PIECE, PIECE), PIECE)
            total = sum_all[rows, :]
            start = pl.multiple_of(n * PACK, 16)
            out[pl.ds(start, PIECE), :] = (acc[rows, :] / total).astype(bf16)
            lse = top_all[rows, :] * SCALE + jnp.log(total)
            out[pl.ds(start + PIECE, STAT), :] = pack_lse(to_lanes(lse, diag))
            return carry

        lax.fori_loop(0, NEAR, finish, 0, unroll=2)


def merge_kernel(a, b, c, d, *outs):
    diag = diagonal()
    refs = (a, b, c, d)
    for n, out in enumerate(outs):
        body = slice(n * PACK, n * PACK + PIECE)
        stat = slice(n * PACK + PIECE, (n + 1) * PACK)
        merged, lse = merge(
            [lambda ref=ref: ref[body, :].astype(f32) for ref in refs],
            [unpack_lse(ref[stat, :]) for ref in refs],
            diag,
        )
        out[0:PIECE, :] = merged.astype(bf16)
        out[PIECE:PACK, :] = pack_lse(lse)


def final_kernel(*refs):
    parts, (own, own_lse, attn, attn_low, lse_out, rows) = refs[:NEAR], refs[NEAR:]
    diag = diagonal()
    merged, lse = merge(
        [lambda ref=ref: ref[0:PIECE, :].astype(f32) for ref in parts] + [lambda: own[...]],
        [unpack_lse(ref[PIECE:PACK, :]) for ref in parts] + [own_lse[0:1, :]],
        diag,
    )
    rows[...] = merged
    lse_out[...] = jnp.broadcast_to(lse, lse_out.shape)
    for s in range(STEPS):
        for h in range(GROUP):
            attn[s * OWN:(s + 1) * OWN, h * HD:(h + 1) * HD] = rows[
                pl.ds(s * GROUP + h, OWN, stride=REQ_ROWS), :
            ]
    attn_low[...] = attn[...].astype(bf16)


def project_kernel(where_ref, pair_ref, here_ref, there_ref, *refs):
    weights, outs, terms = refs[:NX], refs[NX:-1], refs[-1]
    one = STEPS * OWN
    pair, here, there = [ref[...].astype(f32) for ref in (pair_ref, here_ref, there_ref)]
    first = where_ref[1] == 0
    low, high = jnp.where(first, here, there), jnp.where(first, there, here)
    left = [pair[:one]]
    other = [pair[one:]]
    for source in (low, high):
        own_side = [source[2 * n * one:(2 * n + 1) * one] for n in range(NEAR - 1)]
        other_side = [source[(2 * n + 1) * one:(2 * n + 2) * one] for n in range(NEAR - 1)]
        swapped = first if source is high else jnp.logical_not(first)
        for a, b in zip(own_side, other_side):
            left.append(jnp.where(swapped, b, a))
            other.append(jnp.where(swapped, a, b))
        if source is low:
            left.append(here[2 * (NEAR - 1) * one:])
            other.append(there[2 * (NEAR - 1) * one:])
    left = jnp.concatenate(left + other, 0).astype(bf16)
    every = nt(left, jnp.concatenate([weight[...] for weight in weights], 0))
    count, columns = every.shape[0] // 2, every.shape[1] // NX
    for n in range(NX):
        term = every[:, n * columns:(n + 1) * columns]
        terms[n] = jnp.concatenate([term[:count], term[count:]], 1)
    for n, out in enumerate(outs):
        out[...] = terms[where_ref[0] ^ n]


def gather_kernel(where_ref, a, b, c, d, out):
    total = a[...] + b[...] + c[...] + d[...]
    columns = out.shape[2]
    first = where_ref[1] == 0
    low = jnp.where(first, total[:, :columns], total[:, columns:])
    high = jnp.where(first, total[:, columns:], total[:, :columns])
    for n in range(NZ):
        for s in range(STEPS):
            rows = slice(n * STEPS * OWN + s * OWN, n * STEPS * OWN + (s + 1) * OWN)
            pair = jnp.concatenate([low[rows], high[rows]], 0)
            place = pl.multiple_of((where_ref[0] ^ n) * 2 * OWN, 2 * OWN)
            out[s, pl.ds(place, 2 * OWN), :] = pair


def plan(request_branch, branch_blocks, block_slot, x, z, core):
    leaf = (x * NZ + z) * 2 + core
    here = SLOTS
    block_ids = jnp.arange(block_slot.shape[0], dtype=jnp.int32)
    j = jnp.arange(CHUNKS * SLOTS, dtype=jnp.int32)
    slot_ids = (leaf ^ (j >> 3)) * here + (j & (here - 1))
    slot_block = jnp.sum(
        jnp.where(block_slot[:, None] == slot_ids[None, :], block_ids[:, None], 0), axis=0
    )
    k = jnp.arange(branch_blocks.shape[0], dtype=jnp.int32)
    cum_end = jnp.sum(jnp.where(k[:, None] <= k[None, :], branch_blocks[:, None], 0), axis=0)
    slot_branch = jnp.sum((cum_end[None, :] <= slot_block[:, None]).astype(jnp.int32), axis=1)
    n = jnp.arange(LOCAL, dtype=jnp.int32)
    owner = ((x ^ (n >> 4)) * NZ + (z ^ (((n >> 2) & (NEAR - 1)) * 2))) * 2 + core
    request = owner * OWN + (n & (OWN - 1))
    every = jnp.arange(request_branch.shape[0], dtype=jnp.int32)
    branch = jnp.sum(jnp.where(request[:, None] == every[None, :], request_branch[None, :], 0), 1)
    before = (branch[None, :] < branch[:, None]) | (
        (branch[None, :] == branch[:, None]) & (n[None, :] < n[:, None])
    )
    rank = jnp.sum(before.astype(jnp.int32), axis=1)
    ordered = jnp.sum(jnp.where(rank[:, None] == n[None, :], n[:, None], 0), axis=0)
    count = jnp.sum((slot_branch[:, None] == branch[None, :]).astype(jnp.int32), axis=1)
    start = jnp.sum((branch[None, :] < slot_branch[:, None]).astype(jnp.int32), axis=1)
    return [
        jnp.concatenate([ordered, count[half], start[half]]).astype(jnp.int32)
        for half in (slice(0, SLOTS), slice(SLOTS, CHUNKS * SLOTS))
    ]


def struct(shape, dtype):
    return jax.ShapeDtypeStruct(shape, dtype)


def shards(
    queries,
    query_gain,
    new_keys,
    new_values,
    root_keys,
    root_values,
    branch_keys,
    branch_values,
    suffix_keys,
    suffix_values,
    out_weight,
    request_branch,
    branch_blocks,
    suffix_length,
    block_slot,
):
    kv, x, z, core = (lax.axis_index(name) for name in ("kv", "x", "z", "core"))
    normed = pl.pallas_call(
        norm_kernel,
        out_shape=struct((PIECE, HD), bf16),
        in_specs=[VMEM, VMEM],
        out_specs=VMEM,
        scratch_shapes=[pltpu.VMEM((PIECE, HD), f32)],
    )(queries.reshape(STEPS, OWN, GROUP * HD), query_gain.reshape(1, HD))
    root = jnp.concatenate([root_keys.reshape(ROOT, HD), root_values.reshape(ROOT, HD)], 0)
    limb = jnp.concatenate([branch_keys.reshape(HELD, HD), branch_values.reshape(HELD, HD)], 0)
    side_root, limb = lax.optimization_barrier((swap(root, "core", 2, 1), limb))
    far_root, far = swap(root, "z", NZ, 1), swap(limb, "z", NZ, 1)
    near = jnp.concatenate([normed] + [swap(normed, "z", NZ, 2 * k) for k in range(1, NEAR)], 0)
    quarters = [near] + [swap(near, "x", NX, k) for k in range(1, NX)]

    roots = [root, far_root, side_root, swap(far_root, "core", 2, 1)]
    quarters[2], side = lax.optimization_barrier((quarters[2], limb))
    side = swap(side, "core", 2, 1)
    meta = plan(request_branch, branch_blocks, block_slot, x, z, core)

    rows = LOCAL * REQ_ROWS
    spare = rows + REQ_ROWS
    state = [struct((spare, HD), bf16)] + [struct((spare, HD), f32)] * 3

    def scratch(count):
        most = count * SLOTS * LOCAL // ITEM + BATCH
        lists = [pltpu.SMEM((most,), jnp.int32)] * 2
        parts = [pltpu.VMEM((BATCH, ITEM * REQ_ROWS, HD), f32)] * 3
        held = [pltpu.VMEM((count * 2 * HELD, HD), bf16)]
        return lists + held + parts + [pltpu.SemaphoreType.DMA((CHUNKS + 3,))]

    cost = pl.CostEstimate(
        flops=4 * rows * HD * 2048, bytes_accessed=8 << 20, transcendentals=rows * 2048
    )
    before = pl.pallas_call(
        functools.partial(shared_kernel, False),
        out_shape=state,
        in_specs=[SMEM] + [ANY] + [VMEM] * (NX + CHUNKS),
        out_specs=[VMEM] * 4,
        scratch_shapes=scratch(1),
        compiler_params=PARAMS,
        cost_estimate=cost,
    )(meta[0], limb, *quarters, *roots)
    turned = out_weight.T
    weights = [turned] + [swap(turned, "x", NX, k) for k in range(1, NX)]
    before, weights, tied = lax.optimization_barrier((before, weights, normed))
    own, own_lse = pl.pallas_call(
        own_kernel,
        out_shape=[struct((PIECE, HD), f32), struct((8, PIECE), f32)],
        in_specs=[SMEM] + [VMEM] * 5,
        out_specs=[VMEM, VMEM],
        compiler_params=PARAMS,
    )(
        suffix_length,
        tied,
        suffix_keys.reshape(OWN, SUF, HD),
        suffix_values.reshape(OWN, SUF, HD),
        new_keys.reshape(STEPS * OWN, HD),
        new_values.reshape(STEPS * OWN, HD),
    )

    far, own, own_lse = lax.optimization_barrier((far, own, own_lse))
    limbs = [side, far, swap(far, "core", 2, 1)]
    partials = pl.pallas_call(
        functools.partial(shared_kernel, True),
        out_shape=[struct((NEAR * PACK, HD), bf16)] * NX,
        in_specs=[SMEM] + [ANY] * (CHUNKS + 3),
        out_specs=[VMEM] * NX,
        scratch_shapes=[pltpu.VMEM(part.shape, part.dtype) for part in state] + scratch(CHUNKS - 1),
        compiler_params=PARAMS,
        cost_estimate=cost,
    )(meta[1], *limbs, *before)
    returned = [partials[0]] + [swap(partials[k], "x", NX, k) for k in (2, 1, 3)]
    merged = pl.pallas_call(
        merge_kernel,
        out_shape=[struct((PACK, HD), bf16)] * NEAR,
        in_specs=[VMEM] * NX,
        out_specs=[VMEM] * NEAR,
        compiler_params=PARAMS,
    )(*returned)
    landed = [merged[0]] + [swap(merged[k], "z", NZ, 2 * k) for k in (2, 1, 3)]
    attn, attn_low, lse = pl.pallas_call(
        final_kernel,
        out_shape=[
            struct((STEPS * OWN, GROUP * HD), f32),
            struct((STEPS * OWN, GROUP * HD), bf16),
            struct((8, PIECE), f32),
        ],
        in_specs=[VMEM] * (NEAR + 2),
        out_specs=[VMEM] * 3,
        scratch_shapes=[pltpu.VMEM((PIECE, HD), f32)],
        compiler_params=PARAMS,
    )(*landed, own, own_lse)
    attn_out = attn.reshape(STEPS, OWN, 1, GROUP * HD)
    log_total = lse[0].reshape(OWN, STEPS, GROUP).transpose(1, 0, 2).reshape(STEPS, OWN, 1, GROUP)

    pair = jnp.concatenate([attn_low, swap(attn_low, "core", 2, 1)], 0)
    fetched = []
    for k in range(1, NEAR):
        moves = [(a * 2 + c, (a ^ (k + NEAR * c)) * 2 + c) for a in range(NZ) for c in range(2)]
        fetched.append(lax.ppermute(pair, ("z", "core"), moves))
    opposite = swap(attn_low, "z", NZ, NEAR)
    fetched = jnp.concatenate(fetched + [opposite], 0)
    rows = [pair, fetched, swap(fetched, "core", 2, 1)]
    columns = out_weight.shape[1]
    term = struct((NZ * STEPS * OWN, 2 * columns), f32)
    terms = pl.pallas_call(
        project_kernel,
        out_shape=[term] * NX,
        in_specs=[SMEM] + [VMEM] * (3 + NX),
        out_specs=[VMEM] * NX,
        scratch_shapes=[pltpu.VMEM((NX,) + term.shape, f32)],
        compiler_params=PARAMS,
    )(jnp.stack([x ^ kv, core]), *rows, *weights)
    arrived = []
    for k in range(NX):
        pairs = [(v * NX + c, c * NX + (v ^ k)) for v in range(NX) for c in range(NX)]
        arrived.append(lax.ppermute(terms[k], ("kv", "x"), pairs))
    layer_out = pl.pallas_call(
        gather_kernel,
        out_shape=struct((STEPS, NZ * 2 * OWN, columns), f32),
        in_specs=[SMEM] + [VMEM] * NX,
        out_specs=VMEM,
        compiler_params=PARAMS,
    )(jnp.stack([z, core]), *arrived)
    return attn_out, log_total, layer_out


def solution(mesh):
    fine = Mesh(mesh.devices.reshape(4, NX, NZ, 2), ("kv", "x", "z", "core"))
    leaf = ("x", "z", "core")
    in_specs = (
        P(None, leaf, "kv", None),
        P(),
        P(None, leaf, "kv", None),
        P(None, leaf, "kv", None),
        P(leaf, "kv", None),
        P(leaf, "kv", None),
        P(leaf, "kv", None),
        P(leaf, "kv", None),
        P(leaf, None, "kv", None),
        P(leaf, None, "kv", None),
        P("kv", leaf),
        P(),
        P(),
        P(leaf),
        P(),
    )
    out_specs = (P(None, leaf, "kv", None), P(None, leaf, "kv", None), P(None, "kv", leaf))
    return jax.shard_map(shards, mesh=fine, in_specs=in_specs, out_specs=out_specs, check_vma=False)
```
